32 devices in a mesh: wa: 2 (over x), uv: 16 (over z, y, core).
Axes of the slice: x: 2, y: 2, z: 4, core: 2. Of those that a mesh axis runs over, the one named last changes fastest.
Arguments:
- visibility: bfloat16 [1536, 2, 256], P(('wa', 'uv')), may hold values from -6 to 6
- coords: bfloat16 [1536, 2, 256], P(('wa', 'uv')), may hold values from -24 to 24
- tile_row: int32 [1536, 1], P(('wa', 'uv')), may hold values from 0 to 63; in each aligned block of 48 rows (0 to 47, 48 to 95, ...) at most 2 rows name the same one
- col_offset: int32 [1536], P(('wa', 'uv')), may hold values from 0 to 4032
- live_count: int32 [2, 16], P('wa', 'uv'), may hold values from 1 to 48, 480 in all within a row
Outputs:
- sky_image: float32 [4096, 4096], P('uv', 'wa')
The draws below stay inside these ranges and needn't reach their ends.
Inputs may be any that keep to these rules, and one draw needn't show every extreme that they name: `tile_row`: within the blocks of one device, at most 2 name the same tile row, and some device reaches 2. A device's live blocks are its first live_count ones; in each w group the 16 counts sum to 480, and the largest count is 48.
All inputs are finite; a program needn't handle non-finite values.
Results may differ from the reference program's by a relative error of at most 0.0069.
Values may be sent and summed in bfloat16 or wider, within the bound.
A program may use at most 128 MiB of HBM per device.

```python
import math
import jax
import jax.numpy as jnp
import numpy as np
from jax import lax

G = 4096
SUB = 64
B_DEV = 48
CAP = 2
K = 256
BLOCKS = 1536
N_WA = 2
N_UV = 16


def plant(array, rng, low, top_value):
    shape = array.shape
    index_at = [jax.random.randint(jax.random.fold_in(rng, axis), (), 0, shape[axis]) for axis in range(len(shape))]
    array = array.at[tuple(index_at)].set(low)
    longest = shape.index(max(shape))
    index_at[longest] = (index_at[longest] + 1) % shape[longest]
    return array.at[tuple(index_at)].set(top_value)


def shard_levels(stream_key, dims, split, least, largest):
    level = 1.0
    for dim, parts in split:
        heights = jax.random.uniform(jax.random.fold_in(jax.random.fold_in(stream_key, 6), dim), (parts,), jnp.float32, least / len(split), largest / len(split))
        level = level * jnp.repeat(jnp.exp(heights), dims[dim] // parts).reshape((-1,) + (1,) * (len(dims) - 1 - dim))
    return level


def length_profile(number_of, total, reach, slope):
    portions = [(1 << 20) // math.isqrt(standing ** slope) + 1 for standing in range(2, number_of + 1)]
    rest, holding = total - reach - (number_of - 1), [1] * (number_of - 1)
    while rest > 0:
        free = [i for i in range(number_of - 1) if holding[i] < reach]
        whole, left = sum([portions[i] for i in free]), rest
        for i in free:
            extra = min(reach - holding[i], max(1, left * portions[i] // whole), rest)
            holding[i] = holding[i] + extra
            rest = rest - extra
    return np.array([reach] + holding)


def uneven(stream_key, count, total, bound, skew):
    if count == 2:
        one = jax.random.randint(stream_key, (), max(1, total - bound), min(bound, total - 1) + 1)
        return jnp.stack([one, total - one])
    sizes = jnp.asarray(length_profile(count, total, bound, skew), jnp.int32)
    couples = (count - 1) // 2
    giver, sink = sizes[1:1 + 2 * couples:2], sizes[2:2 + 2 * couples:2]
    slack = jnp.minimum(giver - 1, bound - sink)
    shifted = jax.random.randint(jax.random.fold_in(stream_key, 1), (couples,), 0, 1 << 20) % (slack + 1)
    sizes = sizes.at[1:1 + 2 * couples:2].set(giver - shifted).at[2:2 + 2 * couples:2].set(sink + shifted)
    return sizes[jax.random.permutation(jax.random.fold_in(stream_key, 2), count)]


def deal_out(stream_key, own, number, rows, count, top, most, lean):
    sequence = jax.random.permutation(stream_key, count)
    heavy_load, ordinary = shares(count, rows * top, most, lean, True), shares(count, rows * top, most, lean, False)
    places = jnp.arange(count)

    def named(sizes, offset_by):
        used = int((sizes > 0).sum())
        fixed = max(1, used // 4)
        shifted = fixed + (places - fixed + offset_by * (used - fixed)) % max(1, count - fixed)
        return jnp.zeros((count,), jnp.int32).at[sequence[jnp.where(places < fixed, places, shifted)]].set(jnp.asarray(sizes, jnp.int32))

    sizes = jnp.where(number % 4 == 0, named(heavy_load, number // 4), named(ordinary, number - number // 4 - 1))
    mixed = jax.random.permutation(jax.random.fold_in(own, 3), count)
    donor, receiver = mixed[0:count // 2 * 2:2], mixed[1:count // 2 * 2:2]
    margin = jnp.minimum(sizes[donor] - 1, most - sizes[receiver]) // 2
    margin = jnp.where((donor == sequence[0]) | (receiver == sequence[0]) | (sizes[receiver] == 0), 0, jnp.maximum(margin, 0))
    shifted = jax.random.randint(jax.random.fold_in(own, 4), (count // 2,), 0, 1 << 20) % (margin + 1)
    sizes = sizes.at[donor].add(-shifted).at[receiver].add(shifted)
    members = jnp.searchsorted(jnp.cumsum(sizes), jnp.arange(rows * top), side="right").astype(jnp.int32)
    listing = members.reshape(top, rows).T
    listing = listing[jax.random.permutation(jax.random.fold_in(own, 1), rows)]
    offset_by = jax.random.randint(jax.random.fold_in(own, 2), (rows, 1), 0, top)
    return jnp.take_along_axis(listing, (jnp.arange(top)[None, :] + offset_by) % top, axis=1)


def shares(number_of, total, reach, slope, full):
    weights = [(1 << 20) // math.isqrt(standing ** slope) + 1 for standing in range(1, number_of + 1)]
    largest = reach if full else min(reach, max(-(-total // number_of), total * weights[0] // sum(weights)))
    least = 1 if total - largest >= number_of - 1 else 0
    counts, rest = [largest] + [least] * (number_of - 1), total - largest - least * (number_of - 1)
    while rest > 0:
        movable = [i for i in range(1, number_of) if counts[i] < largest] or [i for i in range(1, number_of) if counts[i] < reach]
        mass, budget = sum([weights[i] for i in movable]), rest
        for i in movable:
            more = min(reach - counts[i], max(1, budget * weights[i] // mass), rest)
            counts[i] = counts[i] + more
            rest = rest - more
    return np.array(counts)


def centred(key, dims, spread, reach, pieces=(), dtype=jnp.bfloat16):
    drawn = spread * jax.random.normal(key, dims, jnp.float32)
    if pieces:
        drawn = drawn * shard_levels(key, dims, pieces, -0.22, 0.18)
    return jnp.clip(drawn, -reach, reach).astype(dtype)


def setup_inputs(seed: int = 0) -> dict:
    keys = jax.random.split(jax.random.key(seed), 6)
    visibility = centred(keys[0], (BLOCKS, 2, K), 1.0, 6.0, ((0, 32),))
    coords = jnp.clip(jax.random.uniform(keys[1], (BLOCKS, 2, K), jnp.float32, -24.0, 24.0) * shard_levels(keys[1], (BLOCKS, 2, K), ((0, 32),), -0.4, 0.0), -24.0, 24.0).astype(jnp.bfloat16)
    tile_row_keys = jax.random.split(jax.random.fold_in(keys[2], 1), BLOCKS // B_DEV)
    tile_row_turns = jax.random.permutation(jax.random.fold_in(keys[2], 3), BLOCKS // B_DEV)
    tile_row = jax.vmap(lambda own, number: deal_out(jax.random.fold_in(keys[2], 2), own, number, B_DEV, G // SUB, 1, CAP, 2))(tile_row_keys, tile_row_turns).reshape((BLOCKS, 1))
    col_offset = plant(jax.random.randint(keys[3], (BLOCKS,), 0, G - SUB + 1), jax.random.fold_in(keys[3], 1), 0, G - SUB).astype(jnp.int32)
    live_count = jax.vmap(lambda own: uneven(own, N_UV, 5 * B_DEV * N_UV // 8, B_DEV, 2))(jax.random.split(keys[4], N_WA)).reshape((N_WA, N_UV)).astype(jnp.int32)
    return {"visibility": visibility, "coords": coords, "tile_row": tile_row, "col_offset": col_offset, "live_count": live_count}


full_turn = 2.0 * math.pi
plane_step = 6.0

def centered(length):
    return (jnp.arange(length) - length // 2).astype(jnp.float32)

def subgrid_angles(coord_col, side_len):
    return full_turn / side_len * (centered(side_len)[None, :, None] * coord_col[:, None, :])

def fourier_pair(side_len):
    offsets = (jnp.arange(side_len) - side_len // 2).astype(jnp.int32)
    product = jnp.mod(offsets[:, None] * offsets[None, :], side_len)
    angles = full_turn / side_len * product.astype(jnp.float32)
    return (jnp.cos(angles), -jnp.sin(angles))

def multiply(einsum_form, first, second):
    return jnp.einsum(einsum_form, first.astype(jnp.float32), second.astype(jnp.float32), precision=lax.Precision.HIGHEST)

def make_subgrids(samples, coords):
    norm_scale = 1.0 / math.sqrt(samples.shape[2])
    angle_u = subgrid_angles(coords[:, 0, :].astype(jnp.float32), SUB)
    angle_v = subgrid_angles(coords[:, 1, :].astype(jnp.float32), SUB)
    cos_u, sin_u = (jnp.cos(angle_u), jnp.sin(angle_u))
    vis_re = samples[:, 0, :].astype(jnp.float32)[:, None, :]
    vis_im = samples[:, 1, :].astype(jnp.float32)[:, None, :]
    left_re = ((vis_re * cos_u - vis_im * sin_u) * norm_scale).astype(jnp.bfloat16)
    left_im = ((vis_re * sin_u + vis_im * cos_u) * norm_scale).astype(jnp.bfloat16)
    right_re = jnp.cos(angle_v).astype(jnp.bfloat16)
    right_im = jnp.sin(angle_v).astype(jnp.bfloat16)
    form_s = 'nlk,nmk->nlm'
    sub_re = (multiply(form_s, left_re, right_re) - multiply(form_s, left_im, right_im)).astype(jnp.bfloat16)
    sub_im = (multiply(form_s, left_re, right_im) + multiply(form_s, left_im, right_re)).astype(jnp.bfloat16)
    four_re, four_im = fourier_pair(SUB)
    four_re = four_re.astype(jnp.bfloat16)
    four_im = four_im.astype(jnp.bfloat16)
    form_a = 'pl,nlm->npm'
    temp_re = (multiply(form_a, four_re, sub_re) - multiply(form_a, four_im, sub_im)).astype(jnp.bfloat16)
    temp_im = (multiply(form_a, four_re, sub_im) + multiply(form_a, four_im, sub_re)).astype(jnp.bfloat16)
    form_b = 'npm,qm->npq'
    out_re = multiply(form_b, temp_re, four_re) - multiply(form_b, temp_im, four_im)
    out_im = multiply(form_b, temp_re, four_im) + multiply(form_b, temp_im, four_re)
    return (jnp.stack([out_re, out_im], axis=1) * (1.0 / SUB)).astype(jnp.bfloat16)

def reference(visibility, coords, tile_row, col_offset, live_count):
    vis_groups = visibility.reshape(N_WA, N_UV, B_DEV, 2, K)
    coord_groups = coords.reshape(N_WA, N_UV, B_DEV, 2, K)
    tile_groups = tile_row.reshape(N_WA, N_UV, B_DEV).astype(jnp.int32)
    col_groups = col_offset.reshape(N_WA, N_UV, B_DEV).astype(jnp.int32)
    checker = (1 - 2 * (jnp.arange(G) % 2)).astype(jnp.float32)
    checker_grid = checker[:, None] * checker[None, :]
    axis_coord = centered(G) / G
    depth_term = jnp.sqrt(1.0 - axis_coord[:, None] ** 2 - axis_coord[None, :] ** 2)
    offsets = jnp.arange(SUB).astype(jnp.int32)

    def per_device(pair_args):
        return make_subgrids(pair_args[0], pair_args[1])

    def fold_group(accumulated, group_args):
        vis_g, coord_g, tile_g, col_g, count_g, group_index = group_args
        built = lax.map(per_device, (vis_g, coord_g))
        live_mask = jnp.arange(B_DEV).astype(jnp.int32)[None, :] < count_g[:, None]
        row_index = tile_g[:, :, None, None] * SUB + offsets[None, None, :, None]
        row_index = jnp.broadcast_to(row_index, (N_UV, B_DEV, SUB, SUB))
        col_index = jnp.broadcast_to(col_g[:, :, None, None] + offsets[None, None, None, :], (N_UV, B_DEV, SUB, SUB))
        row_index = jnp.where(live_mask[:, :, None, None], row_index, G)
        values = jnp.moveaxis(built.astype(jnp.float32), 2, 0)
        plane_grid = jnp.zeros((2, G, G), jnp.float32).at[:, row_index, col_index].add(values, mode='drop')
        spectrum = (plane_grid[0] + 1j * plane_grid[1]) * checker_grid
        plane_image = (jnp.fft.ifft2(spectrum) * G * checker_grid).T
        plane_depth = (group_index.astype(jnp.float32) - (N_WA - 1) / 2.0) * plane_step
        screen_angle = full_turn * plane_depth * (depth_term - 1.0)
        term = jnp.real(plane_image) * jnp.cos(screen_angle) - jnp.imag(plane_image) * jnp.sin(screen_angle)
        return (accumulated + term.astype(jnp.float32), None)
    summed, _ = lax.scan(fold_group, jnp.zeros((G, G), jnp.float32), (vis_groups, coord_groups, tile_groups, col_groups, live_count.astype(jnp.int32), jnp.arange(N_WA).astype(jnp.int32)))
    return summed
```

```python
import functools
import math

import jax
import jax.numpy as jnp
import ml_dtypes
import numpy as np
from jax import lax
from jax.experimental import pallas as pl
from jax.experimental.pallas import tpu as pltpu
from jax.sharding import PartitionSpec as P

G = 4096
SUB = 64
UNROLL = 3
STACK = 4
LANES = 128
PITCH = 129
plane_step = 6.0
full_turn = 2.0 * math.pi
BF = ml_dtypes.bfloat16


def turn_poly():
    nodes = np.cos(np.pi * (np.arange(256) + 0.5) / 256)
    z = (nodes + 1.0) / 8.0
    f = np.sqrt(z)
    cos_c = np.polynomial.chebyshev.cheb2poly(
        np.polynomial.chebyshev.chebfit(nodes, np.cos(2 * np.pi * f), 5)
    )
    sin_c = np.polynomial.chebyshev.cheb2poly(
        np.polynomial.chebyshev.chebfit(nodes, np.sin(2 * np.pi * f) / f, 5)
    )
    base = np.polynomial.Polynomial([-1.0, 8.0])
    out = []
    for coefs in (cos_c, sin_c):
        total = np.polynomial.Polynomial([0.0])
        for c in coefs[::-1]:
            total = total * base + c
        out.append([float(c) for c in total.coef])
    return out


COS_C, SIN_C = turn_poly()


def cos_sin_turns(turns):
    f = turns - jnp.round(turns)
    z = f * f
    c = COS_C[-1] * z + COS_C[-2]
    for k in COS_C[-3::-1]:
        c = c * z + k
    s = SIN_C[-1] * z + SIN_C[-2]
    for k in SIN_C[-3::-1]:
        s = s * z + k
    return c, s * f


def half_orders():
    fine = np.arange(8) + 0.5
    return np.concatenate([fine, 16 - fine, 16 + fine, 32 - fine])


def dirichlet(x):
    bottom = np.sin(np.pi * x / SUB)
    zero = np.abs(bottom) < 1e-12
    return np.where(zero, float(SUB), np.sin(np.pi * x) / np.where(zero, 1.0, bottom))


def spread_table():
    at = (np.arange(G) - G // 2) / SUB + 0.5
    order = half_orders()[:, None]
    minus, plus = dirichlet(at[None] - order), dirichlet(at[None] + order)
    return np.concatenate([minus + plus, minus - plus], axis=0)


def column_table():
    return (spread_table() / SUB).astype(np.float32)


def row_table(parts):
    whole = (spread_table() / G).reshape(SUB, parts, SUB // parts, 64)
    return np.ascontiguousarray(whole.transpose(1, 3, 2, 0)).astype(BF)


def head_matrices():
    l0 = np.arange(64)[:, None]
    out = []
    for core in range(2):
        columns = []
        for source in range(2):
            t = (2 * np.arange(32) + (core ^ source))[None, :]
            ang = full_turn / 64 * np.mod(l0 * t, 64)
            c, s = np.cos(ang), np.sin(ang)
            columns.append(np.block([[c, -s], [s, c]]))
        out.append(np.concatenate(columns, axis=1))
    return np.stack(out).astype(BF)


def gather_kernel(far, near, x_ref, out_ref, z_send, z_recv, y_send, y_recv, c_send, c_recv):
    me = lax.axis_index("uv")
    c = lax.rem(me, 2)
    b = lax.rem(me // 2, near)
    a = me // (2 * near)

    def at(da, db, dc):
        return (
            lax.rem(a + da + far, far) * near + lax.rem(b + db + near, near)
        ) * 2 + lax.rem(c + dc, 2)

    peers = [at(d, 0, 0) for d in range(1, far)]
    peers += [at(0, e, 0) for e in range(1, near)] + [at(0, 0, 1)]
    barrier = pltpu.get_barrier_semaphore()
    for peer in peers:
        pl.semaphore_signal(
            barrier, inc=1, device_id={"uv": peer}, device_id_type=pl.DeviceIdType.MESH
        )
    pl.semaphore_wait(barrier, len(peers))

    def copy(source, slot, target, send, recv):
        return pltpu.make_async_remote_copy(
            src_ref=source,
            dst_ref=out_ref.at[slot],
            send_sem=send,
            recv_sem=recv,
            device_id={"uv": target},
            device_id_type=pl.DeviceIdType.MESH,
        )

    sent = []

    def send(source, slot, target, send_sem, recv_sem):
        one = copy(source, slot, target, send_sem, recv_sem)
        one.start()
        sent.append(one)

    for d in range(1, far):
        send(x_ref, me, at(d, 0, 0), z_send.at[d], z_recv.at[d])
    for d in range(far):
        slot = at(-d, 0, 0)
        source = x_ref if d == 0 else out_ref.at[slot]
        if d > 0:
            copy(x_ref, slot, me, z_send.at[d], z_recv.at[d]).wait_recv()
        for e in range(1, near):
            k = d * near + e
            send(source, slot, at(0, e, 0), y_send.at[k], y_recv.at[k])
        k = d * near
        send(source, slot, at(0, 0, 1), c_send.at[k], c_recv.at[k])
        if d == 0:
            out_ref[me] = x_ref[...]
    for d in range(far):
        for e in range(1, near):
            k = d * near + e
            slot = at(-d, -e, 0)
            copy(x_ref, slot, me, y_send.at[k], y_recv.at[k]).wait_recv()
            send(out_ref.at[slot], slot, at(0, 0, 1), c_send.at[k], c_recv.at[k])
    for d in range(far):
        for e in range(near):
            k = d * near + e
            copy(x_ref, at(-d, -e, 1), me, c_send.at[k], c_recv.at[k]).wait_recv()
    for one in sent:
        one.wait_send()


def gather_all(packed, uv_count):
    chips = uv_count // 2
    near = 1 << ((chips.bit_length() - 1) // 2)
    far = chips // near
    sems = [far] * 2 + [far * near] * 4
    return pl.pallas_call(
        functools.partial(gather_kernel, far, near),
        out_shape=jax.ShapeDtypeStruct((uv_count,) + packed.shape, packed.dtype),
        in_specs=[pl.BlockSpec(memory_space=pltpu.VMEM)],
        out_specs=pl.BlockSpec(memory_space=pltpu.VMEM),
        scratch_shapes=[pltpu.SemaphoreType.DMA((n,)) for n in sems],
        compiler_params=pltpu.CompilerParams(
            collective_id=0, has_side_effects=True, vmem_limit_bytes=24 * 1024 * 1024
        ),
    )(packed)


def grid_kernel(
    width, blocks, homes, data_ref, cols_ref, moff_ref, d_ref,
    keep_ref, give_ref, acc, rows_f, phase, slots, filled, group,
):
    devices = data_ref.shape[0]
    cap = 2 * devices
    half_tiles = G // SUB // 2
    k_len = data_ref.shape[2]
    acc[...] = jnp.zeros_like(acc)

    def empty(h, carry):
        filled[h] = 0
        return carry

    lax.fori_loop(0, half_tiles + 1, empty, 0)

    def spread(j, carry):
        rows_f[j] = data_ref[j].astype(jnp.float32)
        turn = jnp.bitwise_and((2 * cols_ref[j] - (G - SUB + 1)) * moff_ref[...], 2 * G - 1)
        pc, ps = cos_sin_turns(turn.astype(jnp.float32) * (0.5 / G))
        phase[j, 0] = pc
        phase[j, 1] = ps

        for i in range(blocks):
            h = homes[j * blocks + i]
            n = filled[h]
            slots[h * cap + n] = j * blocks + i
            filled[h] = n + 1
        return carry

    lax.fori_loop(0, devices, spread, 0)

    def list_groups(h, found):
        def one(g, n):
            group[3 * n] = h
            group[3 * n + 1] = h * cap + STACK * g
            group[3 * n + 2] = filled[h] - STACK * g
            return n + 1

        return lax.fori_loop(0, (filled[h] + STACK - 1) // STACK, one, found)

    total = lax.fori_loop(0, half_tiles, list_groups, 0)

    sub = lax.broadcasted_iota(jnp.int32, (8, k_len), 0)
    fine = (sub.astype(jnp.float32) + 0.5) * (1.0 / SUB)

    def pick(values):
        out = jnp.zeros((8, k_len), jnp.float32)
        for n, value in enumerate(values):
            if value:
                out = jnp.where(sub == n, value / SUB, out)
        return out

    coarse_u = pick((16.0, 32.0, 0.0, 0.0, -0.5))
    coarse_v = pick((0.0, 0.0, 16.0, 32.0, -0.5))
    scale = 1.0 / math.sqrt(k_len)

    def expand(c, s, c1, s1, c2, s2):
        a, b, d, e = c1 * c, s1 * s, s1 * c, c1 * s
        return (
            jnp.concatenate([c, a + b, a - b, c2 * c + s2 * s], axis=0),
            jnp.concatenate([s, d - e, d + e, s2 * c - c2 * s], axis=0),
        )

    def one_block(j, i, keep):
        vr, vi, u, v = (rows_f[j, pl.ds(q * blocks + i, 1), :] for q in range(4))
        u = u + 0.5
        v = v + 0.5
        cc, cs = cos_sin_turns(coarse_u * u + coarse_v * v)
        row = lambda n: (cc[n : n + 1], cs[n : n + 1])
        cu, su = expand(*cos_sin_turns(fine * u), *row(0), *row(1))
        cv, sv = expand(*cos_sin_turns(fine * v), *row(2), *row(3))
        hc, hs = row(4)
        wr = (vr * hc - vi * hs) * keep
        wi = (vr * hs + vi * hc) * keep
        left = jnp.concatenate([wr * cu, -wi * su, wi * cu, wr * su], axis=0)
        right = jnp.concatenate([cv, sv], axis=0)
        s = lax.dot_general(
            left.astype(jnp.bfloat16),
            right.astype(jnp.bfloat16),
            (((1,), (1,)), ((), ())),
            preferred_element_type=jnp.float32,
        ).astype(jnp.bfloat16)
        return s, phase[j, 0, pl.ds(i, 1), :], phase[j, 1, pl.ds(i, 1), :]

    def step(it, carry):
        for k in range(UNROLL):
            n = it * UNROLL + k
            real = n < total
            n = jnp.where(real, n, 0)
            h = group[3 * n]
            first = group[3 * n + 1]
            left_over = jnp.where(real, group[3 * n + 2], 0)
            made = []
            for q in range(STACK):
                live = q < left_over
                g = jnp.where(live, slots[first + q], 0)
                j = g // blocks
                made.append(one_block(j, g - j * blocks, jnp.where(live, scale, 0.0)))
            piece = jnp.concatenate([s for s, _, _ in made], axis=1)
            rows = pl.ds(h * PITCH, 2 * SUB)
            half = 2 * width
            for lane in range(0, half, min(half, 256)):
                cut = slice(lane, lane + min(half, 256))
                dc, ds = d_ref[:32, cut], d_ref[32:, cut]
                for turn in range(2):
                    weight = []
                    for _, pr, pi in made:
                        pr, pi = pr[:, cut], pi[:, cut]
                        weight += [dc * pi, ds * pr] if turn else [dc * pr, ds * -pi]
                    got = jnp.dot(
                        piece,
                        jnp.concatenate(weight, axis=0).astype(jnp.bfloat16),
                        preferred_element_type=jnp.float32,
                    )
                    for c in range(got.shape[1] // LANES):
                        at = (turn * half + lane) // LANES + c
                        acc[at, rows, :] += got[:, c * LANES : (c + 1) * LANES]
        return carry

    lax.fori_loop(0, (total + UNROLL - 1) // UNROLL, step, 0)

    def turned(lam, carry):
        chunks = 2 * width // LANES
        top = [acc[c, pl.ds(lam, half_tiles, stride=PITCH), :] for c in range(2 * chunks)]
        low = [acc[c, pl.ds(SUB + lam, half_tiles, stride=PITCH), :] for c in range(2 * chunks)]
        re = jnp.concatenate([top[c] - low[chunks + c] for c in range(chunks)], axis=1)
        im = jnp.concatenate([top[chunks + c] + low[c] for c in range(chunks)], axis=1)
        keep_ref[lam] = jnp.concatenate([re[:, :width], im[:, :width]], axis=0).astype(jnp.bfloat16)
        give_ref[lam] = jnp.concatenate([re[:, width:], im[:, width:]], axis=0).astype(jnp.bfloat16)
        return carry

    lax.fori_loop(0, SUB, turned, 0, unroll=4)


def in_lanes(rows):
    width = rows.shape[1]
    if width < LANES:
        return [jnp.concatenate([rows] * (LANES // width), axis=1)]
    return [rows[:, c : c + LANES] for c in range(0, width, LANES)]


def lane_chunks(width):
    return max(1, width // LANES)


def tail_rows(width, share, place, y_of, table, out_t):
    part, depth, m_first = place

    def step(l0, carry):
        z = jnp.dot(table[l0], y_of(l0), preferred_element_type=jnp.float32)
        l1 = part * share + lax.broadcasted_iota(jnp.int32, (share, width), 0)
        l = l0 + 64 * l1 - G // 2
        m = m_first + lax.broadcasted_iota(jnp.int32, (share, width), 1)
        x = l.astype(jnp.float32) * (1.0 / G)
        y = m.astype(jnp.float32) * (1.0 / G)
        ramp = jnp.bitwise_and(-(G - SUB + 1) * l, 2 * G - 1).astype(jnp.float32) * (0.5 / G)
        sc, ss = cos_sin_turns(depth * (jnp.sqrt(1.0 - y * y - x * x) - 1.0) + ramp)
        for c, rows in enumerate(in_lanes(z[:, :width] * sc - z[:, width:] * ss)):
            out_t[c, pl.ds(l0, share, stride=64), :] = rows
        return carry

    lax.fori_loop(0, 64, step, 0, unroll=4)


def turn_out(out_t, out_ref):
    chunk = 128

    def step(n, carry):
        at = pl.multiple_of(n * chunk, chunk)
        for c in range(out_t.shape[0]):
            turned = out_t[c, pl.ds(at, chunk), :].T.astype(out_ref.dtype)
            width = min(LANES, out_ref.shape[0])
            out_ref[c * width : (c + 1) * width, pl.ds(at, chunk)] = turned[:width]
        return carry

    lax.fori_loop(0, out_t.shape[1] // chunk, step, 0, unroll=4)


def head_kernel(
    width, share, places, depths, own_ref, came_ref, head_ref, table, y_ref, out_ref, mid, out_t
):
    def head(lam, carry):
        rhs = jnp.concatenate([own_ref[lam], came_ref[lam]], axis=0)
        got = jnp.dot(head_ref[...], rhs, preferred_element_type=jnp.float32)
        for c, rows in enumerate(in_lanes(got)):
            mid[c, pl.ds(lam * PITCH, 128), :] = rows
        return carry

    lax.fori_loop(0, SUB, head, 0, unroll=4)

    def y_of(l0):
        halves = []
        for first in (0, 64):
            rows = [mid[c, pl.ds(first + l0, SUB, stride=PITCH), :] for c in range(mid.shape[0])]
            halves += [r[:, : min(width, LANES)] for r in rows]
        y = jnp.concatenate(halves, axis=1).astype(jnp.bfloat16)
        y_ref[l0] = y
        return y

    tail_rows(width, share, (places[0], depths[0], places[1]), y_of, table, out_t)
    turn_out(out_t, out_ref)


def tail_kernel(width, share, places, depths, y_ref, table, out_ref, out_t):
    tail_rows(
        width, share, (places[0], depths[0], places[1]), lambda l0: y_ref[l0], table, out_t
    )
    turn_out(out_t, out_ref)


def on_device(visibility, coords, tile_row, col_offset, live_count):
    uv_count = lax.axis_size("uv")
    wa_count = lax.axis_size("wa")
    uv_index = lax.axis_index("uv")
    wa_index = lax.axis_index("wa")
    blocks = visibility.shape[0]
    k_len = visibility.shape[2]
    width = G // uv_count
    core = jnp.mod(uv_index, 2)
    partner = uv_index + 1 - 2 * core
    numbers = jnp.stack(
        [
            tile_row[:, 0],
            col_offset // SUB,
            jnp.mod(col_offset, SUB),
            jnp.broadcast_to(live_count[0], (blocks,)),
        ]
    )
    numbers = jnp.pad(numbers, ((0, 12), (0, k_len - blocks))).astype(jnp.bfloat16)
    packed = jnp.concatenate(
        [visibility[:, 0], visibility[:, 1], coords[:, 0], coords[:, 1], numbers], axis=0
    )
    columns = jnp.asarray(column_table())
    d_table = jnp.concatenate(
        [
            lax.dynamic_slice_in_dim(columns, uv_index * width, width, 1),
            lax.dynamic_slice_in_dim(columns, partner * width, width, 1),
        ],
        axis=1,
    )
    m_first = uv_index * width - G // 2
    m_both = jnp.concatenate(
        [m_first + jnp.arange(width), partner * width + jnp.arange(width) - G // 2]
    )[None, :]
    all_data = gather_all(packed, uv_count)
    came_numbers = all_data[:, 4 * blocks : 4 * blocks + 4, :blocks].astype(jnp.int32)
    tiles = came_numbers[:, 0]
    live = jnp.arange(blocks)[None, :] < came_numbers[:, 3]
    mine = live & (jnp.mod(tiles, 2) == core)
    homes = jnp.where(mine, tiles // 2, G // SUB // 2).reshape(-1)
    cols = (came_numbers[:, 1] * SUB + came_numbers[:, 2])[:, :, None]

    rows = packed.shape[0]
    half_tiles = G // SUB // 2
    cap = 2 * uv_count
    shape = (SUB, SUB, width)
    vmem = pl.BlockSpec(memory_space=pltpu.VMEM)
    smem = pl.BlockSpec(memory_space=pltpu.SMEM)
    own, give = pl.pallas_call(
        functools.partial(grid_kernel, width, blocks),
        out_shape=[jax.ShapeDtypeStruct(shape, jnp.bfloat16)] * 2,
        in_specs=[smem, vmem, vmem, vmem, vmem],
        out_specs=[vmem, vmem],
        scratch_shapes=[
            pltpu.VMEM((4 * width // LANES, half_tiles * PITCH, LANES), jnp.float32),
            pltpu.VMEM((uv_count, rows, k_len), jnp.float32),
            pltpu.VMEM((uv_count, 2, blocks, 2 * width), jnp.float32),
            pltpu.SMEM((half_tiles * cap + uv_count * blocks,), jnp.int32),
            pltpu.SMEM((half_tiles + 1,), jnp.int32),
            pltpu.SMEM((3 * (uv_count * blocks // STACK + half_tiles),), jnp.int32),
        ],
        compiler_params=pltpu.CompilerParams(vmem_limit_bytes=48 * 1024 * 1024),
    )(homes, all_data, cols, m_both, d_table)
    came_half = lax.ppermute(give, "uv", [(n, n ^ 1) for n in range(uv_count)])

    share = 64 // wa_count
    depth = ((wa_index.astype(jnp.float32) - (wa_count - 1) / 2.0) * plane_step)[None]
    tables = jnp.asarray(row_table(wa_count))
    span = G // wa_count

    def places_of(part):
        return jnp.stack([part, m_first]).astype(jnp.int32)

    def head_of(part, dtype):
        return pl.pallas_call(
            functools.partial(head_kernel, width, share),
            out_shape=[
                jax.ShapeDtypeStruct((64, SUB, 2 * width), jnp.bfloat16),
                jax.ShapeDtypeStruct((width, span), dtype),
            ],
            in_specs=[smem, smem, vmem, vmem, vmem, vmem],
            out_specs=[vmem, vmem],
            scratch_shapes=[
                pltpu.VMEM((lane_chunks(width), SUB * PITCH, LANES), jnp.float32),
                pltpu.VMEM((lane_chunks(width), span, LANES), jnp.float32),
            ],
            compiler_params=pltpu.CompilerParams(vmem_limit_bytes=40 * 1024 * 1024),
        )(
            places_of(part), depth, own, came_half, jnp.asarray(head_matrices())[core], tables[part]
        )

    def tail_of(part, first, dtype):
        return pl.pallas_call(
            functools.partial(tail_kernel, width, share),
            out_shape=jax.ShapeDtypeStruct((width, span), dtype),
            in_specs=[smem, smem, vmem, vmem],
            out_specs=vmem,
            scratch_shapes=[pltpu.VMEM((lane_chunks(width), span, LANES), jnp.float32)],
            compiler_params=pltpu.CompilerParams(vmem_limit_bytes=40 * 1024 * 1024),
        )(places_of(part), depth, first, tables[part])

    if wa_count == 2:
        first, away = head_of(1 - wa_index, jnp.bfloat16)
        came = lax.ppermute(away, "wa", [(0, 1), (1, 0)])
        return tail_of(wa_index, first, jnp.float32) + came.astype(jnp.float32)
    first, part = head_of(jnp.int32(0), jnp.bfloat16)
    images = [part] + [tail_of(jnp.int32(n), first, jnp.bfloat16) for n in range(1, wa_count)]
    parts = jnp.stack(images, axis=1)
    came = lax.all_to_all(parts, "wa", split_axis=1, concat_axis=1)
    return jnp.sum(came.astype(jnp.float32), axis=1)


def solution(mesh):
    in_specs = (
        P(("wa", "uv"), None, None),
        P(("wa", "uv"), None, None),
        P(("wa", "uv"), None),
        P(("wa", "uv")),
        P("wa", "uv"),
    )
    return jax.shard_map(
        on_device, mesh=mesh, in_specs=in_specs, out_specs=P("uv", "wa"), check_vma=False
    )
```

```python
import functools
import math

import jax
import jax.numpy as jnp
import ml_dtypes
import numpy as np
from jax import lax
from jax.experimental import pallas as pl
from jax.experimental.pallas import tpu as pltpu
from jax.sharding import PartitionSpec as P

G = 4096
SUB = 64
BATCH = 8
STACK = 4
LANES = 128
PITCH = 129
OUT_PITCH = 65
SWAPS = 2
SENDS = 4
plane_step = 6.0
full_turn = 2.0 * math.pi
BF = ml_dtypes.bfloat16


def turn_poly(bound, degree):
    nodes = np.cos(np.pi * (np.arange(256) + 0.5) / 256)
    z = (nodes + 1.0) / (2.0 * bound)
    f = np.sqrt(z)
    cos_c = np.polynomial.chebyshev.cheb2poly(
        np.polynomial.chebyshev.chebfit(nodes, np.cos(2 * np.pi * f), degree)
    )
    sin_c = np.polynomial.chebyshev.cheb2poly(
        np.polynomial.chebyshev.chebfit(nodes, np.sin(2 * np.pi * f) / f, degree)
    )
    base = np.polynomial.Polynomial([-1.0, 2.0 * bound])
    out = []
    for coefs in (cos_c, sin_c):
        total = np.polynomial.Polynomial([0.0])
        for c in coefs[::-1]:
            total = total * base + c
        out.append([float(c) for c in total.coef])
    return out


COS_C, SIN_C = turn_poly(4.0, 5)
COS_S, SIN_S = turn_poly(16.0, 4)


def cos_sin_part(f, cos_c, sin_c):
    z = f * f
    c = cos_c[-1] * z + cos_c[-2]
    for k in cos_c[-3::-1]:
        c = c * z + k
    s = sin_c[-1] * z + sin_c[-2]
    for k in sin_c[-3::-1]:
        s = s * z + k
    return c, s * f


def cos_sin_turns(turns):
    return cos_sin_part(turns - jnp.round(turns), COS_C, SIN_C)


def times(a, b):
    return a[0] * b[0] - a[1] * b[1], a[0] * b[1] + a[1] * b[0]


def squared(a):
    twice = a[0] + a[0]
    return twice * a[0] - 1.0, twice * a[1]


def half_orders():
    fine = np.arange(8) + 0.5
    return np.concatenate([fine, 16 - fine, 16 + fine, 32 - fine])


def dirichlet(x):
    bottom = np.sin(np.pi * x / SUB)
    zero = np.abs(bottom) < 1e-12
    return np.where(zero, float(SUB), np.sin(np.pi * x) / np.where(zero, 1.0, bottom))


def spread_table():
    at = (np.arange(G) - G // 2) / SUB + 0.5
    order = half_orders()[:, None]
    minus, plus = dirichlet(at[None] - order), dirichlet(at[None] + order)
    return np.concatenate([minus + plus, minus - plus], axis=0)


def column_table(devices):
    whole = (spread_table() / SUB).reshape(SUB, devices, G // devices)
    return np.ascontiguousarray(whole.transpose(1, 0, 2)).astype(np.float32)


def row_table(parts):
    whole = (spread_table() / G).reshape(SUB, parts, SUB // parts, 64)
    return np.ascontiguousarray(whole.transpose(1, 3, 2, 0)).astype(BF)


def head_matrices():
    l0 = np.arange(64)[:, None]
    out = []
    for core in range(2):
        columns = []
        for source in range(2):
            t = (2 * np.arange(32) + (core ^ source))[None, :]
            ang = full_turn / 64 * np.mod(l0 * t, 64)
            c, s = np.cos(ang), np.sin(ang)
            columns.append(np.block([[c, -s], [s, c]]))
        out.append(np.concatenate(columns, axis=1))
    return np.stack(out).astype(BF)


def gather_kernel(far, near, x_ref, out_ref, z_send, z_recv, y_send, y_recv, c_send, c_recv):
    me = lax.axis_index("uv")
    c = lax.rem(me, 2)
    b = lax.rem(me // 2, near)
    a = me // (2 * near)

    def at(da, db, dc):
        return (
            lax.rem(a + da + far, far) * near + lax.rem(b + db + near, near)
        ) * 2 + lax.rem(c + dc, 2)

    peers = [at(d, 0, 0) for d in range(1, far)]
    peers += [at(0, e, 0) for e in range(1, near)] + [at(0, 0, 1)]
    barrier = pltpu.get_barrier_semaphore()
    for peer in peers:
        pl.semaphore_signal(
            barrier, inc=1, device_id={"uv": peer}, device_id_type=pl.DeviceIdType.MESH
        )
    pl.semaphore_wait(barrier, len(peers))

    def copy(source, slot, target, send, recv):
        return pltpu.make_async_remote_copy(
            src_ref=source,
            dst_ref=out_ref.at[slot],
            send_sem=send,
            recv_sem=recv,
            device_id={"uv": target},
            device_id_type=pl.DeviceIdType.MESH,
        )

    sent = []

    def send(source, slot, target, send_sem, recv_sem):
        one = copy(source, slot, target, send_sem, recv_sem)
        one.start()
        sent.append(one)

    for d in range(1, far):
        send(x_ref, me, at(d, 0, 0), z_send.at[d], z_recv.at[d])
    for d in range(far):
        slot = at(-d, 0, 0)
        source = x_ref if d == 0 else out_ref.at[slot]
        if d > 0:
            copy(x_ref, slot, me, z_send.at[d], z_recv.at[d]).wait_recv()
        for e in range(1, near):
            k = d * near + e
            send(source, slot, at(0, e, 0), y_send.at[k], y_recv.at[k])
        k = d * near
        send(source, slot, at(0, 0, 1), c_send.at[k], c_recv.at[k])
        if d == 0:
            out_ref[me] = x_ref[...]
    for d in range(far):
        for e in range(1, near):
            k = d * near + e
            slot = at(-d, -e, 0)
            copy(x_ref, slot, me, y_send.at[k], y_recv.at[k]).wait_recv()
            send(out_ref.at[slot], slot, at(0, 0, 1), c_send.at[k], c_recv.at[k])
    for d in range(far):
        for e in range(near):
            k = d * near + e
            copy(x_ref, at(-d, -e, 1), me, c_send.at[k], c_recv.at[k]).wait_recv()
    for one in sent:
        one.wait_send()


def gather_all(packed, uv_count):
    chips = uv_count // 2
    near = 1 << ((chips.bit_length() - 1) // 2)
    far = chips // near
    sems = [far] * 2 + [far * near] * 4
    return pl.pallas_call(
        functools.partial(gather_kernel, far, near),
        out_shape=jax.ShapeDtypeStruct((uv_count,) + packed.shape, packed.dtype),
        in_specs=[pl.BlockSpec(memory_space=pltpu.VMEM)],
        out_specs=pl.BlockSpec(memory_space=pltpu.VMEM),
        scratch_shapes=[pltpu.SemaphoreType.DMA((n,)) for n in sems],
        compiler_params=pltpu.CompilerParams(
            collective_id=0, has_side_effects=True, vmem_limit_bytes=24 * 1024 * 1024
        ),
    )(packed)


def grid_kernel(
    width, blocks, k_len, homes, data_ref, cols_ref, m_ref, d_all, keep_ref, give_ref,
    acc, rows_f, slots, filled, group, d_ref, *buffers,
):
    devices = data_ref.shape[0]
    cap = 2 * devices
    half_tiles = G // SUB // 2
    both = 2 * width
    k_parts = k_len // LANES
    m_parts = both // LANES
    each = 5 * blocks
    uv = lax.axis_index("uv")
    stage = buffers[0]
    sets = (buffers[1:5], buffers[5:9])
    d_ref[:, :width] = d_all[uv]
    d_ref[:, width:] = d_all[uv + 1 - 2 * lax.rem(uv, 2)]

    def empty(h, carry):
        filled[h] = 0
        return carry

    lax.fori_loop(0, half_tiles + 1, empty, 0)
    clear = max(1, half_tiles // devices) * PITCH

    def spread(j, carry):
        at = jnp.minimum(j * clear, half_tiles * PITCH - clear)
        for c in range(2 * m_parts):
            acc[c, pl.ds(at, clear), :] = jnp.zeros((clear, LANES), jnp.float32)
        base = pl.multiple_of(j * each, 8)
        for c in range(k_parts):
            rows_f[c, pl.ds(base, 4 * blocks), :] = data_ref[
                j, : 4 * blocks, c * LANES : (c + 1) * LANES
            ].astype(jnp.float32)
        rows_f[0, pl.ds(base + 4 * blocks, blocks), :] = jnp.broadcast_to(
            cols_ref[j], (blocks, LANES)
        )
        for i in range(blocks):
            h = homes[j * blocks + i]
            n = filled[h]
            slots[h * cap + n] = j * each + i
            filled[h] = n + 1
        return carry

    lax.fori_loop(0, devices, spread, 0)

    def list_groups(h, found):
        def one(g, n):
            group[3 * n] = h
            group[3 * n + 1] = h * cap + STACK * g
            group[3 * n + 2] = filled[h] - STACK * g
            return n + 1

        return lax.fori_loop(0, (filled[h] + STACK - 1) // STACK, one, found)

    total = lax.fori_loop(0, half_tiles, list_groups, 0)
    scale = 1.0 / math.sqrt(k_len)

    def prepare(batch, refs):
        fine, coarse, signal, phase = refs
        for p in range(BATCH // STACK):
            n = batch * (BATCH // STACK) + p
            real = n < total
            n = jnp.where(real, n, 0)
            first = group[3 * n + 1]
            left_over = jnp.where(real, group[3 * n + 2], 0)
            for q in range(STACK):
                live = q < left_over
                row = jnp.where(live, slots[first + q], 0)
                keep = jnp.where(live, scale, 0.0)
                k = p * STACK + q
                for c in range(k_parts):
                    for r in range(4):
                        value = rows_f[c, pl.ds(row + r * blocks, 1), :]
                        stage[r, c, k : k + 1, :] = value * keep if r < 2 else value
                stage[4, 0, k : k + 1, :] = rows_f[0, pl.ds(row + 4 * blocks, 1), :]
        for c in range(k_parts):
            halves = []
            for axis in range(2):
                turns = (stage[2 + axis, c] + 0.5) * (0.5 / SUB)
                half = cos_sin_part(turns, COS_S, SIN_S)
                halves.append(half)
                step = squared(half)
                power = half
                for b in range(8):
                    if b:
                        power = times(power, step)
                    for e in range(2):
                        fine[axis, e, c, b * 9 : b * 9 + 8, :] = power[e]
                power = squared(times(power, half))
                for e in range(2):
                    coarse[4 * axis + e, c] = power[e]
                power = squared(power)
                for e in range(2):
                    coarse[4 * axis + 2 + e, c] = power[e]
            hc, hs = times(*halves)
            vr, vi = stage[0, c], stage[1, c]
            signal[0, c] = vr * hc + vi * hs
            wi = vi * hc - vr * hs
            signal[1, c] = wi
            signal[2, c] = -wi
        for c in range(m_parts):
            pc, ps = cos_sin_turns(stage[4, 0] * m_ref[:, c * LANES : (c + 1) * LANES])
            phase[0, c] = pc
            phase[1, c] = ps
            phase[2, c] = -ps

    def expand(c, s, c1, s1, c2, s2):
        a, b, d, e = c1 * c, s1 * s, s1 * c, c1 * s
        return (
            jnp.concatenate([c, a + b, a - b, c2 * c + s2 * s], axis=0),
            jnp.concatenate([s, d - e, d + e, s2 * c - c2 * s], axis=0),
        )

    def piece_of(k, refs):
        fine, coarse, signal, _ = refs
        lefts, rights = [], []
        for c in range(k_parts):
            tables = []
            for axis in range(2):
                start = [fine[axis, e, c, pl.ds(k, 8, stride=9), :] for e in range(2)]
                rows = [coarse[4 * axis + n, c, k : k + 1, :] for n in range(4)]
                tables.append(expand(*start, *rows))
            (cu, su), (cv, sv) = tables
            wr, wi, nwi = (signal[n, c, k : k + 1, :] for n in range(3))
            lefts.append(
                jnp.concatenate([wr * cu, nwi * su, wi * cu, wr * su], axis=0).astype(jnp.bfloat16)
            )
            rights.append(jnp.concatenate([cv, sv], axis=0).astype(jnp.bfloat16))
        return lax.dot_general(
            jnp.concatenate(lefts, axis=1),
            jnp.concatenate(rights, axis=1),
            (((1,), (1,)), ((), ())),
            preferred_element_type=jnp.float32,
        ).astype(jnp.bfloat16)

    def gather_up(batch, refs):
        phase = refs[3]
        for p in range(BATCH // STACK):
            n = batch * (BATCH // STACK) + p
            h = group[3 * jnp.where(n < total, n, 0)]
            rows = pl.ds(h * PITCH, 2 * SUB)
            ks = range(p * STACK, (p + 1) * STACK)
            piece = jnp.concatenate([piece_of(k, refs) for k in ks], axis=1)
            wide = min(2, m_parts)
            for c0 in range(0, m_parts, wide):
                for turn in range(2):
                    weight = []
                    for k in ks:
                        top, low = [], []
                        for c in range(c0, c0 + wide):
                            cut = slice(c * LANES, (c + 1) * LANES)
                            pr, pi, npi = (phase[e, c, k : k + 1, :] for e in range(3))
                            top.append(d_ref[:32, cut] * (pi if turn else pr))
                            low.append(d_ref[32:, cut] * (pr if turn else npi))
                        weight += [jnp.concatenate(top, axis=1), jnp.concatenate(low, axis=1)]
                    got = jnp.dot(
                        piece,
                        jnp.concatenate(weight, axis=0).astype(jnp.bfloat16),
                        preferred_element_type=jnp.float32,
                    )
                    for c in range(wide):
                        at = turn * m_parts + c0 + c
                        acc[at, rows, :] += got[:, c * LANES : (c + 1) * LANES]

    batches = (total + BATCH // STACK - 1) // (BATCH // STACK)
    prepare(0, sets[0])

    def step(it, carry):
        for n in range(2):
            gather_up(2 * it + n, sets[n])
            prepare(2 * it + n + 1, sets[1 - n])
        return carry

    lax.fori_loop(0, (batches + 1) // 2, step, 0)

    def turned(lam, carry):
        top = [acc[c, pl.ds(lam, half_tiles, stride=PITCH), :] for c in range(2 * m_parts)]
        low = [acc[c, pl.ds(SUB + lam, half_tiles, stride=PITCH), :] for c in range(2 * m_parts)]
        re = [top[c] - low[m_parts + c] for c in range(m_parts)]
        im = [top[m_parts + c] + low[c] for c in range(m_parts)]
        if width < LANES:
            re = [re[0][:, :width], re[0][:, width:]]
            im = [im[0][:, :width], im[0][:, width:]]
        whole = [jnp.concatenate(x, axis=0).astype(jnp.bfloat16) for x in zip(re, im)]
        parts = len(whole) // 2
        for c in range(parts):
            keep_ref[c, lam] = whole[c]
            give_ref[c, lam] = whole[parts + c]
        return carry

    lax.fori_loop(0, SUB, turned, 0, unroll=4)


def in_lanes(rows):
    width = rows.shape[1]
    if width < LANES:
        return [jnp.concatenate([rows] * (LANES // width), axis=1)]
    return [rows[:, c : c + LANES] for c in range(0, width, LANES)]


def lane_chunks(width):
    return max(1, width // LANES)


def tail_rows(width, share, place, y_of, table, out_t):
    part, depth, m_first = place

    def step(l0, carry):
        z = jnp.dot(table[l0], y_of(l0), preferred_element_type=jnp.float32)
        l1 = part * share + lax.broadcasted_iota(jnp.int32, (share, width), 0)
        l = l0 + 64 * l1 - G // 2
        m = m_first + lax.broadcasted_iota(jnp.int32, (share, width), 1)
        x = l.astype(jnp.float32) * (1.0 / G)
        y = m.astype(jnp.float32) * (1.0 / G)
        ramp = jnp.bitwise_and(-(G - SUB + 1) * l, 2 * G - 1).astype(jnp.float32) * (0.5 / G)
        sc, ss = cos_sin_turns(depth * (jnp.sqrt(1.0 - y * y - x * x) - 1.0) + ramp)
        for c, rows in enumerate(in_lanes(z[:, :width] * sc - z[:, width:] * ss)):
            out_t[c, pl.ds(l0, share, stride=64), :] = rows
        return carry

    lax.fori_loop(0, 64, step, 0, unroll=4)


def turn_out(out_t, out_ref):
    chunk = 128

    def step(n, carry):
        at = pl.multiple_of(n * chunk, chunk)
        for c in range(out_t.shape[0]):
            turned = out_t[c, pl.ds(at, chunk), :].T.astype(out_ref.dtype)
            width = min(LANES, out_ref.shape[0])
            out_ref[c * width : (c + 1) * width, pl.ds(at, chunk)] = turned[:width]
        return carry

    lax.fori_loop(0, out_t.shape[1] // chunk, step, 0, unroll=4)


def head_kernel(
    width, share, places, depths, own_ref, came_ref, head_ref, table, y_ref, out_ref, mid, out_t
):
    def head(lam, carry):
        rhs = jnp.concatenate([own_ref[0, lam], came_ref[0, lam]], axis=0)
        got = jnp.dot(head_ref[...], rhs, preferred_element_type=jnp.float32)
        for c, rows in enumerate(in_lanes(got)):
            mid[c, pl.ds(lam * PITCH, 128), :] = rows
        return carry

    lax.fori_loop(0, SUB, head, 0, unroll=4)

    def y_of(l0):
        halves = []
        for first in (0, 64):
            rows = [mid[c, pl.ds(first + l0, SUB, stride=PITCH), :] for c in range(mid.shape[0])]
            halves += [r[:, : min(width, LANES)] for r in rows]
        y = jnp.concatenate(halves, axis=1).astype(jnp.bfloat16)
        y_ref[l0] = y
        return y

    tail_rows(width, share, (places[0], depths[0], places[1]), y_of, table, out_t)
    turn_out(out_t, out_ref)


def tail_kernel(width, share, places, depths, y_ref, table, out_ref, out_t):
    tail_rows(
        width, share, (places[0], depths[0], places[1]), lambda l0: y_ref[l0], table, out_t
    )
    turn_out(out_t, out_ref)


def finish_kernel(
    width, places, depths, keep_ref, give_ref, head_all, table,
    out_ref, came, mid, y_buf, away, other, out_t, core_send, core_recv, far_send, far_recv,
):
    uv = lax.axis_index("uv")
    wa = lax.axis_index("wa")
    near = {"uv": uv + 1 - 2 * lax.rem(uv, 2)}
    far = {"wa": 1 - wa}
    mesh_type = pl.DeviceIdType.MESH
    barrier = pltpu.get_barrier_semaphore()
    pl.semaphore_signal(barrier, inc=1, device_id=near, device_id_type=mesh_type)
    pl.semaphore_signal(barrier, inc=1, device_id=far, device_id_type=mesh_type)
    pl.semaphore_wait(barrier, 2)

    parts = width // LANES
    lam_step = SUB // SWAPS
    swaps = []
    for c in range(parts):
        for k in range(SWAPS):
            at = pl.ds(k * lam_step, lam_step)
            n = c * SWAPS + k
            swaps.append(
                pltpu.make_async_remote_copy(
                    src_ref=give_ref.at[c, at],
                    dst_ref=came.at[c, at],
                    send_sem=core_send.at[n],
                    recv_sem=core_recv.at[n],
                    device_id=near,
                    device_id_type=mesh_type,
                )
            )
            swaps[-1].start()
    core = lax.rem(uv, 2)

    share = SUB // 2
    step = 64 // SENDS

    def screened(c, l0, part, z):
        l1 = part * share + lax.broadcasted_iota(jnp.int32, (share, LANES), 0)
        l = l0 + 64 * l1 - G // 2
        m = places[1] + c * LANES + lax.broadcasted_iota(jnp.int32, (share, LANES), 1)
        x = l.astype(jnp.float32) * (1.0 / G)
        y = m.astype(jnp.float32) * (1.0 / G)
        ramp = jnp.bitwise_and(-(G - SUB + 1) * l, 2 * G - 1).astype(jnp.float32) * (0.5 / G)
        sc, ss = cos_sin_turns(depths[0] * (jnp.sqrt(1.0 - y * y - x * x) - 1.0) + ramp)
        return z[:, :LANES] * sc - z[:, LANES:] * ss

    sends = []
    for c in range(parts):

        def head(lam, carry, c=c):
            rhs = jnp.concatenate([keep_ref[c, lam], came[c, lam]], axis=0)
            mid[c, pl.ds(lam * PITCH, 128), :] = jnp.dot(
                head_all[core], rhs, preferred_element_type=jnp.float32
            )
            return carry

        for k in range(SWAPS):
            swaps[c * SWAPS + k].wait_recv()
            lax.fori_loop(k * lam_step, (k + 1) * lam_step, head, 0, unroll=4)

        def away_rows(l0, carry, c=c):
            y = jnp.concatenate(
                [mid[c, pl.ds(first + l0, SUB, stride=PITCH), :] for first in (0, 64)], axis=1
            ).astype(jnp.bfloat16)
            y_buf[c, l0] = y
            z = jnp.dot(table[1 - wa, l0], y, preferred_element_type=jnp.float32)
            away[c, l0] = screened(c, l0, 1 - places[0], z).astype(jnp.bfloat16)
            return carry

        for k in range(SENDS):
            lax.fori_loop(k * step, (k + 1) * step, away_rows, 0, unroll=4)
            at = pl.ds(k * step, step)
            n = c * SENDS + k
            sends.append(
                pltpu.make_async_remote_copy(
                    src_ref=away.at[c, at],
                    dst_ref=other.at[c, at],
                    send_sem=far_send.at[n],
                    recv_sem=far_recv.at[n],
                    device_id=far,
                    device_id_type=mesh_type,
                )
            )
            sends[-1].start()

    for c in range(parts):

        def own_rows(l0, carry, c=c):
            z = jnp.dot(table[wa, l0], y_buf[c, l0], preferred_element_type=jnp.float32)
            out_t[c, pl.ds(l0, share, stride=OUT_PITCH), :] = screened(c, l0, places[0], z)
            return carry

        lax.fori_loop(0, 64, own_rows, 0, unroll=4)

    for c in range(parts):

        def add_rows(l0, carry, c=c):
            at = pl.ds(l0, share, stride=OUT_PITCH)
            out_t[c, at, :] += other[c, l0].astype(jnp.float32)
            return carry

        for k in range(SENDS):
            sends[c * SENDS + k].wait_recv()
            lax.fori_loop(k * step, (k + 1) * step, add_rows, 0, unroll=4)

        for n in range(share // 2):
            rows = [out_t[c, pl.ds((2 * n + h) * OUT_PITCH, 64), :] for h in range(2)]
            out_ref[c * LANES : (c + 1) * LANES, n * LANES : (n + 1) * LANES] = jnp.concatenate(
                rows, axis=0
            ).T
    for one in swaps + sends:
        one.wait_send()


def on_device(visibility, coords, tile_row, col_offset, live_count):
    uv_count = lax.axis_size("uv")
    wa_count = lax.axis_size("wa")
    uv_index = lax.axis_index("uv")
    wa_index = lax.axis_index("wa")
    blocks = visibility.shape[0]
    k_len = visibility.shape[2]
    width = G // uv_count
    core = jnp.mod(uv_index, 2)
    partner = uv_index + 1 - 2 * core
    numbers = jnp.stack(
        [
            tile_row[:, 0],
            col_offset // SUB,
            jnp.mod(col_offset, SUB),
            jnp.broadcast_to(live_count[0], (blocks,)),
        ]
    )
    numbers = jnp.pad(numbers, ((0, 12), (0, k_len - blocks))).astype(jnp.bfloat16)
    packed = jnp.concatenate(
        [visibility[:, 0], visibility[:, 1], coords[:, 0], coords[:, 1], numbers], axis=0
    )
    m_first = uv_index * width - G // 2
    m_both = jnp.concatenate(
        [m_first + jnp.arange(width), partner * width + jnp.arange(width) - G // 2]
    )[None, :].astype(jnp.float32) * (0.5 / G)
    all_data = gather_all(packed, uv_count)
    came_numbers = all_data[:, 4 * blocks : 4 * blocks + 4, :blocks].astype(jnp.int32)
    tiles = came_numbers[:, 0]
    live = jnp.arange(blocks)[None, :] < came_numbers[:, 3]
    mine = live & (jnp.mod(tiles, 2) == core)
    homes = jnp.where(mine, tiles // 2, G // SUB // 2).reshape(-1)
    cols = 2 * (came_numbers[:, 1] * SUB + came_numbers[:, 2]) - (G - SUB + 1)
    cols = cols[:, :, None].astype(jnp.float32)

    half_tiles = G // SUB // 2
    cap = 2 * uv_count
    shape = (lane_chunks(width), SUB, SUB, min(width, LANES))
    vmem = pl.BlockSpec(memory_space=pltpu.VMEM)
    smem = pl.BlockSpec(memory_space=pltpu.SMEM)
    m_parts = 2 * width // LANES
    k_parts = k_len // LANES
    buffers = [
        pltpu.VMEM((2, 2, k_parts, 72, LANES), jnp.float32),
        pltpu.VMEM((8, k_parts, BATCH, LANES), jnp.float32),
        pltpu.VMEM((3, k_parts, BATCH, LANES), jnp.float32),
        pltpu.VMEM((3, m_parts, BATCH, LANES), jnp.float32),
    ]
    own, give = pl.pallas_call(
        functools.partial(grid_kernel, width, blocks, k_len),
        out_shape=[jax.ShapeDtypeStruct(shape, jnp.bfloat16)] * 2,
        in_specs=[smem, vmem, vmem, vmem, vmem],
        out_specs=[vmem, vmem],
        scratch_shapes=[
            pltpu.VMEM((2 * m_parts, half_tiles * PITCH, LANES), jnp.float32),
            pltpu.VMEM((k_parts, uv_count * 5 * blocks, LANES), jnp.float32),
            pltpu.SMEM((half_tiles * cap + uv_count * blocks,), jnp.int32),
            pltpu.SMEM((half_tiles + 1,), jnp.int32),
            pltpu.SMEM((3 * (uv_count * blocks // STACK + half_tiles),), jnp.int32),
            pltpu.VMEM((SUB, 2 * width), jnp.float32),
            pltpu.VMEM((5, k_parts, BATCH, LANES), jnp.float32),
        ]
        + buffers
        + buffers,
        compiler_params=pltpu.CompilerParams(vmem_limit_bytes=32 * 1024 * 1024),
    )(homes, all_data, cols, m_both, jnp.asarray(column_table(uv_count)))
    share = 64 // wa_count
    depth = ((wa_index.astype(jnp.float32) - (wa_count - 1) / 2.0) * plane_step)[None]
    tables = jnp.asarray(row_table(wa_count))
    span = G // wa_count

    def places_of(part):
        return jnp.stack([part, m_first]).astype(jnp.int32)

    def head_of(part, dtype):
        return pl.pallas_call(
            functools.partial(head_kernel, width, share),
            out_shape=[
                jax.ShapeDtypeStruct((64, SUB, 2 * width), jnp.bfloat16),
                jax.ShapeDtypeStruct((width, span), dtype),
            ],
            in_specs=[smem, smem, vmem, vmem, vmem, vmem],
            out_specs=[vmem, vmem],
            scratch_shapes=[
                pltpu.VMEM((lane_chunks(width), SUB * PITCH, LANES), jnp.float32),
                pltpu.VMEM((lane_chunks(width), span, LANES), jnp.float32),
            ],
            compiler_params=pltpu.CompilerParams(vmem_limit_bytes=40 * 1024 * 1024),
        )(
            places_of(part), depth, own, came_half, jnp.asarray(head_matrices())[core], tables[part]
        )

    def tail_of(part, first, dtype):
        return pl.pallas_call(
            functools.partial(tail_kernel, width, share),
            out_shape=jax.ShapeDtypeStruct((width, span), dtype),
            in_specs=[smem, smem, vmem, vmem],
            out_specs=vmem,
            scratch_shapes=[pltpu.VMEM((lane_chunks(width), span, LANES), jnp.float32)],
            compiler_params=pltpu.CompilerParams(vmem_limit_bytes=40 * 1024 * 1024),
        )(places_of(part), depth, first, tables[part])

    if wa_count == 2 and width % LANES == 0:
        parts = width // LANES
        scratch = [
            pltpu.VMEM(shape, jnp.bfloat16),
            pltpu.VMEM((parts, SUB * PITCH, LANES), jnp.float32),
            pltpu.VMEM((parts, 64, SUB, 2 * LANES), jnp.bfloat16),
            pltpu.VMEM((parts, 64, share, LANES), jnp.bfloat16),
            pltpu.VMEM((parts, 64, share, LANES), jnp.bfloat16),
            pltpu.VMEM((parts, share * OUT_PITCH, LANES), jnp.float32),
        ]
        scratch += [pltpu.SemaphoreType.DMA((parts * SWAPS,))] * 2
        scratch += [pltpu.SemaphoreType.DMA((parts * SENDS,))] * 2
        return pl.pallas_call(
            functools.partial(finish_kernel, width),
            out_shape=jax.ShapeDtypeStruct((width, span), jnp.float32),
            in_specs=[smem, smem] + [vmem] * 4,
            out_specs=vmem,
            scratch_shapes=scratch,
            compiler_params=pltpu.CompilerParams(
                collective_id=1, has_side_effects=True, vmem_limit_bytes=24 * 1024 * 1024
            ),
        )(
            places_of(wa_index),
            depth,
            own,
            give,
            jnp.asarray(head_matrices()),
            tables,
        )
    came_half = lax.ppermute(give, "uv", [(n, n ^ 1) for n in range(uv_count)])

    first, part = head_of(jnp.int32(0), jnp.bfloat16)
    images = [part] + [tail_of(jnp.int32(n), first, jnp.bfloat16) for n in range(1, wa_count)]
    parts = jnp.stack(images, axis=1)
    came = lax.all_to_all(parts, "wa", split_axis=1, concat_axis=1)
    return jnp.sum(came.astype(jnp.float32), axis=1)


def solution(mesh):
    in_specs = (
        P(("wa", "uv"), None, None),
        P(("wa", "uv"), None, None),
        P(("wa", "uv"), None),
        P(("wa", "uv")),
        P("wa", "uv"),
    )
    return jax.shard_map(
        on_device, mesh=mesh, in_specs=in_specs, out_specs=P("uv", "wa"), check_vma=False
    )
```

```python
import functools
import math

import jax
import jax.numpy as jnp
import ml_dtypes
import numpy as np
from jax import lax
from jax.experimental import pallas as pl
from jax.experimental.pallas import tpu as pltpu
from jax.sharding import PartitionSpec as P

G = 4096
SUB = 64
BATCH = 8
PLACES = 8
STACK = 4
LANES = 128
PITCH = 129
OUT_PITCH = 65
SWAPS = 2
SENDS = 4
plane_step = 6.0
full_turn = 2.0 * math.pi
BF = ml_dtypes.bfloat16


def turn_poly(bound, degree):
    nodes = np.cos(np.pi * (np.arange(256) + 0.5) / 256)
    z = (nodes + 1.0) / (2.0 * bound)
    f = np.sqrt(z)
    cos_c = np.polynomial.chebyshev.cheb2poly(
        np.polynomial.chebyshev.chebfit(nodes, np.cos(2 * np.pi * f), degree)
    )
    sin_c = np.polynomial.chebyshev.cheb2poly(
        np.polynomial.chebyshev.chebfit(nodes, np.sin(2 * np.pi * f) / f, degree)
    )
    base = np.polynomial.Polynomial([-1.0, 2.0 * bound])
    out = []
    for coefs in (cos_c, sin_c):
        total = np.polynomial.Polynomial([0.0])
        for c in coefs[::-1]:
            total = total * base + c
        out.append([float(c) for c in total.coef])
    return out


COS_C, SIN_C = turn_poly(4.0, 5)
COS_S, SIN_S = turn_poly(16.0, 4)


def cos_sin_part(f, cos_c, sin_c):
    z = f * f
    c = cos_c[-1] * z + cos_c[-2]
    for k in cos_c[-3::-1]:
        c = c * z + k
    s = sin_c[-1] * z + sin_c[-2]
    for k in sin_c[-3::-1]:
        s = s * z + k
    return c, s * f


def cos_sin_turns(turns):
    return cos_sin_part(turns - jnp.round(turns), COS_C, SIN_C)


def times(a, b):
    return a[0] * b[0] - a[1] * b[1], a[0] * b[1] + a[1] * b[0]


def squared(a):
    twice = a[0] + a[0]
    return twice * a[0] - 1.0, twice * a[1]


def half_orders():
    fine = np.arange(8) + 0.5
    return np.concatenate([fine, 16 - fine, 16 + fine, 32 - fine])


def dirichlet(x):
    bottom = np.sin(np.pi * x / SUB)
    zero = np.abs(bottom) < 1e-12
    return np.where(zero, float(SUB), np.sin(np.pi * x) / np.where(zero, 1.0, bottom))


def spread_table():
    at = (np.arange(G) - G // 2) / SUB + 0.5
    order = half_orders()[:, None]
    minus, plus = dirichlet(at[None] - order), dirichlet(at[None] + order)
    return np.concatenate([minus + plus, minus - plus], axis=0)


def column_table(devices):
    whole = (spread_table() / SUB).reshape(SUB, devices, G // devices)
    return np.ascontiguousarray(whole.transpose(1, 0, 2)).astype(np.float32)


def row_table(parts):
    whole = (spread_table() / G).reshape(SUB, parts, SUB // parts, 64)
    return np.ascontiguousarray(whole.transpose(1, 3, 2, 0)).astype(BF)


def head_matrices():
    l0 = np.arange(64)[:, None]
    out = []
    for core in range(2):
        columns = []
        for source in range(2):
            t = (2 * np.arange(32) + (core ^ source))[None, :]
            ang = full_turn / 64 * np.mod(l0 * t, 64)
            c, s = np.cos(ang), np.sin(ang)
            columns.append(np.block([[c, -s], [s, c]]))
        out.append(np.concatenate(columns, axis=1))
    return np.stack(out).astype(BF)


def gather_kernel(
    far, near, x_ref, out_ref,
    own_sem, ring_send, ring_recv, side_send, side_recv, core_send, core_recv,
):
    uv = lax.axis_index("uv")
    c = lax.rem(uv, 2)
    b = lax.rem(uv // 2, near)
    a = uv // (2 * near)
    mesh_type = pl.DeviceIdType.MESH
    sources = (x_ref,)
    outs = (out_ref,)

    def at(da, db, dc):
        return ((a + da) * near + lax.rem(b + db + near, near)) * 2 + lax.rem(c + dc, 2)

    def inside(da):
        return jnp.logical_and(a + da >= 0, a + da < far)

    barrier = pltpu.get_barrier_semaphore()

    def greet(device):
        pl.semaphore_signal(barrier, inc=1, device_id={"uv": device}, device_id_type=mesh_type)

    for side in (-1, 1):
        pl.when(inside(side))(lambda side=side: greet(at(side, 0, 0)))
    for e in range(1, near):
        greet(at(0, e, 0))
    greet(at(0, 0, 1))
    mine = [
        pltpu.make_async_copy(sources[k], outs[k].at[uv], own_sem.at[k]) for k in range(1)
    ]
    for one in mine:
        one.start()
    beside = jnp.where(a > 0, 1, 0) + jnp.where(a < far - 1, 1, 0)
    pl.semaphore_wait(barrier, beside + near)

    def copy(k, own, slot, target, send, recv):
        return pltpu.make_async_remote_copy(
            src_ref=sources[k] if own else outs[k].at[slot],
            dst_ref=outs[k].at[slot],
            send_sem=send,
            recv_sem=recv,
            device_id={"uv": target},
            device_id_type=mesh_type,
        )

    first = (0,)
    second = ()
    sends = []

    def start(valid, one):
        pl.when(valid)(lambda: one.start())
        sends.append((valid, one))

    def along(k, da, e, own):
        slot = at(da, -e, 0)
        if da <= 0:
            n = (k * near + e) * 2 * far - da
            start(
                jnp.logical_and(inside(da), inside(1)),
                copy(k, own, slot, at(1, 0, 0), ring_send.at[n], ring_recv.at[n + 1]),
            )
        if da >= 0:
            n = ((k * near + e) * 2 + 1) * far + da
            start(
                jnp.logical_and(inside(da), inside(-1)),
                copy(k, own, slot, at(-1, 0, 0), ring_send.at[n], ring_recv.at[n + 1]),
            )

    def arrived_along(k, da, e):
        slot = at(da, -e, 0)
        n = (k * near + e) * 2 * far - da if da < 0 else ((k * near + e) * 2 + 1) * far + da
        one = copy(k, False, slot, uv ^ 1, ring_send.at[n], ring_recv.at[n])
        pl.when(inside(da))(lambda: one.wait_recv())

    def aside(k, da, own):
        for e in range(1, near):
            n = (k * (2 * far) + far + da) * near + e
            start(
                inside(da),
                copy(k, own, at(da, 0, 0), at(0, e, 0), side_send.at[n], side_recv.at[n]),
            )

    def arrived_aside(k, da, e):
        n = (k * (2 * far) + far + da) * near + e
        one = copy(k, False, at(da, -e, 0), uv ^ 1, side_send.at[n], side_recv.at[n])
        pl.when(inside(da))(lambda: one.wait_recv())

    def across(k, da, e, own):
        n = (k * (2 * far) + far + da) * near + e
        start(
            inside(da),
            copy(k, own, at(da, -e, 0), at(0, 0, 1), core_send.at[n], core_recv.at[n]),
        )

    for k in second:
        aside(k, 0, True)
    for k in first:
        along(k, 0, 0, True)
    for k in second:
        along(k, 0, 0, True)
    for k in first:
        aside(k, 0, True)
    for k in range(1):
        across(k, 0, 0, True)
    for e in range(1, near):
        for k in second:
            arrived_aside(k, 0, e)
            along(k, 0, e, False)
            across(k, 0, e, False)
    for s in range(1, far):
        for k in first:
            for da in (-s, s):
                arrived_along(k, da, 0)
                along(k, da, 0, False)
                aside(k, da, False)
                across(k, da, 0, False)
        for e in range(near):
            for k in second:
                for da in (-s, s):
                    arrived_along(k, da, e)
                    along(k, da, e, False)
                    across(k, da, e, False)
    for k in first:
        for da in sorted(range(1 - far, far), key=abs):
            for e in range(1, near):
                arrived_aside(k, da, e)
                across(k, da, e, False)
    for da in sorted(range(1 - far, far), key=abs):
        for e in range(near):
            for k in range(1):
                n = (k * (2 * far) + far + da) * near + e
                one = copy(k, False, at(da, -e, 1), uv ^ 1, core_send.at[n], core_recv.at[n])
                pl.when(inside(da))(lambda one=one: one.wait_recv())
    for one in mine:
        one.wait()
    for valid, one in sends:
        pl.when(valid)(lambda one=one: one.wait_send())


def gather_all(packed, uv_count):
    chips = uv_count // 2
    near = 1 << ((chips.bit_length() - 1) // 2)
    far = chips // near
    sems = [1] + [near * 2 * far + 1] * 2 + [2 * far * near] * 4
    return pl.pallas_call(
        functools.partial(gather_kernel, far, near),
        out_shape=jax.ShapeDtypeStruct((uv_count,) + packed.shape, packed.dtype),
        in_specs=[pl.BlockSpec(memory_space=pltpu.VMEM)],
        out_specs=pl.BlockSpec(memory_space=pltpu.VMEM),
        scratch_shapes=[pltpu.SemaphoreType.DMA((n,)) for n in sems],
        compiler_params=pltpu.CompilerParams(
            collective_id=0, has_side_effects=True, vmem_limit_bytes=16 * 1024 * 1024
        ),
    )(packed)


def grid_kernel(
    width, blocks, homes, cols, counts, data_ref, m_ref, d_all, keep_ref, give_ref,
    acc, slots, filled, fours, twos, d_ref, *buffers,
):
    each = 2 * blocks + 2
    devices = data_ref.shape[0] // each
    k_len = data_ref.shape[2]
    cap = 2 * devices
    half_tiles = G // SUB // 2
    both = 2 * width
    k_parts = k_len // LANES
    m_parts = both // LANES
    uv = lax.axis_index("uv")
    stage = buffers[0]
    sets = (buffers[1:5], buffers[5:9])
    d_ref[:, :width] = d_all[uv]
    d_ref[:, width:] = d_all[uv + 1 - 2 * lax.rem(uv, 2)]

    for n in range(3):
        fours[n] = 0
        twos[n] = 0

    def empty(h, carry):
        filled[h] = 0
        return carry

    lax.fori_loop(0, half_tiles + 1, empty, 0)
    clear = max(1, half_tiles // devices) * PITCH

    def spread(j, carry):
        at = jnp.minimum(j * clear, half_tiles * PITCH - clear)
        for c in range(2 * m_parts):
            acc[c, pl.ds(at, clear), :] = jnp.zeros((clear, LANES), jnp.float32)
        def place(n, inner):
            for k in range(PLACES):
                i = n * PLACES + k
                h = homes[j * blocks + i]
                n_h = filled[h]
                slots[h * cap + n_h] = j * each + i
                filled[h] = n_h + 1
            return inner

        return lax.fori_loop(0, (counts[j] + PLACES - 1) // PLACES, place, carry)

    lax.fori_loop(0, devices, spread, 0)

    def list_groups(h, found):
        count = filled[h]
        whole = (count + 1) // STACK

        def one(g, n):
            fours[3 * n] = h
            fours[3 * n + 1] = h * cap + STACK * g
            fours[3 * n + 2] = count - STACK * g
            return n + 1

        n, m = found
        n = lax.fori_loop(0, whole, one, n)
        rest = count - STACK * whole
        twos[3 * m] = h
        twos[3 * m + 1] = h * cap + STACK * whole
        twos[3 * m + 2] = rest
        return n, m + jnp.where(rest > 0, 1, 0)

    n_fours, n_twos = lax.fori_loop(0, half_tiles, list_groups, (0, 0))
    scale = 1.0 / math.sqrt(k_len)

    def prepare(batch, refs, stack, group, total):
        fine, coarse, signal, phase = refs
        for p in range(BATCH // stack):
            n = batch * (BATCH // stack) + p
            real = n < total
            n = jnp.where(real, n, 0)
            first = group[3 * n + 1]
            left_over = jnp.where(real, group[3 * n + 2], 0)
            for q in range(stack):
                live = q < left_over
                row = jnp.where(live, slots[first + q], 0)
                centre = (2 * cols[row] - (G - SUB + 1)).astype(jnp.float32)
                keep = jnp.where(live, scale, 0.0)
                k = p * stack + q
                signals = data_ref[row].astype(jnp.float32) * keep
                places = data_ref[row + blocks].astype(jnp.float32)
                for c in range(k_parts):
                    cut = slice(c * LANES, (c + 1) * LANES)
                    for r in range(2):
                        stage[r, c, k : k + 1, :] = signals[r : r + 1, cut]
                        stage[2 + r, c, k : k + 1, :] = places[r : r + 1, cut]
                stage[4, 0, k : k + 1, :] = jnp.full((1, LANES), centre, jnp.float32)
        for c in range(k_parts):
            halves = []
            for axis in range(2):
                turns = (stage[2 + axis, c] + 0.5) * (0.5 / SUB)
                half = cos_sin_part(turns, COS_S, SIN_S)
                halves.append(half)
                step = squared(half)
                power = half
                for b in range(8):
                    if b:
                        power = times(power, step)
                    for e in range(2):
                        fine[axis, e, c, b * 9 : b * 9 + 8, :] = power[e]
                power = squared(times(power, half))
                for e in range(2):
                    coarse[4 * axis + e, c] = power[e]
                power = squared(power)
                for e in range(2):
                    coarse[4 * axis + 2 + e, c] = power[e]
            hc, hs = times(*halves)
            vr, vi = stage[0, c], stage[1, c]
            signal[0, c] = vr * hc + vi * hs
            wi = vi * hc - vr * hs
            signal[1, c] = wi
            signal[2, c] = -wi
        for c in range(m_parts):
            pc, ps = cos_sin_turns(stage[4, 0] * m_ref[:, c * LANES : (c + 1) * LANES])
            phase[0, c] = pc
            phase[1, c] = ps
            phase[2, c] = -ps

    def expand(c, s, c1, s1, c2, s2):
        a, b, d, e = c1 * c, s1 * s, s1 * c, c1 * s
        return (
            jnp.concatenate([c, a + b, a - b, c2 * c + s2 * s], axis=0),
            jnp.concatenate([s, d - e, d + e, s2 * c - c2 * s], axis=0),
        )

    def piece_of(k, refs):
        fine, coarse, signal, _ = refs
        lefts, rights = [], []
        for c in range(k_parts):
            tables = []
            for axis in range(2):
                start = [fine[axis, e, c, pl.ds(k, 8, stride=9), :] for e in range(2)]
                rows = [coarse[4 * axis + n, c, k : k + 1, :] for n in range(4)]
                tables.append(expand(*start, *rows))
            (cu, su), (cv, sv) = tables
            wr, wi, nwi = (signal[n, c, k : k + 1, :] for n in range(3))
            lefts.append(
                jnp.concatenate([wr * cu, nwi * su, wi * cu, wr * su], axis=0).astype(jnp.bfloat16)
            )
            rights.append(jnp.concatenate([cv, sv], axis=0).astype(jnp.bfloat16))
        return lax.dot_general(
            jnp.concatenate(lefts, axis=1),
            jnp.concatenate(rights, axis=1),
            (((1,), (1,)), ((), ())),
            preferred_element_type=jnp.float32,
        ).astype(jnp.bfloat16)

    def gather_up(batch, refs, stack, group, total):
        phase = refs[3]
        pieces = [
            jnp.concatenate([piece_of(k, refs) for k in range(p * stack, (p + 1) * stack)], axis=1)
            for p in range(BATCH // stack)
        ]
        for p in range(BATCH // stack):
            n = batch * (BATCH // stack) + p
            h = group[3 * jnp.where(n < total, n, 0)]
            rows = pl.ds(h * PITCH, 2 * SUB)
            ks = range(p * stack, (p + 1) * stack)
            piece = pieces[p]
            wide = min(2, m_parts)
            for c0 in range(0, m_parts, wide):
                tops = [d_ref[:32, c * LANES : (c + 1) * LANES] for c in range(c0, c0 + wide)]
                lows = [d_ref[32:, c * LANES : (c + 1) * LANES] for c in range(c0, c0 + wide)]
                for turn in range(2):
                    weight = []
                    for k in ks:
                        top, low = [], []
                        for c in range(c0, c0 + wide):
                            pr, pi, npi = (phase[e, c, k : k + 1, :] for e in range(3))
                            top.append(tops[c - c0] * (pi if turn else pr))
                            low.append(lows[c - c0] * (pr if turn else npi))
                        weight += [jnp.concatenate(top, axis=1), jnp.concatenate(low, axis=1)]
                    got = jnp.dot(
                        piece,
                        jnp.concatenate(weight, axis=0).astype(jnp.bfloat16),
                        preferred_element_type=jnp.float32,
                    )
                    for c in range(wide):
                        at = turn * m_parts + c0 + c
                        acc[at, rows, :] += got[:, c * LANES : (c + 1) * LANES]

    for stack, group, total in ((STACK, fours, n_fours), (2, twos, n_twos)):
        batches = (total + BATCH // stack - 1) // (BATCH // stack)
        rest = (stack, group, total)
        prepare(0, sets[0], *rest)

        def step(it, carry, rest=rest):
            for n in range(2):
                gather_up(2 * it + n, sets[n], *rest)
                prepare(2 * it + n + 1, sets[1 - n], *rest)
            return carry

        lax.fori_loop(0, batches // 2, step, 0)

        def last(it, carry, rest=rest, batches=batches):
            gather_up(batches - 1, sets[0], *rest)
            return carry

        lax.fori_loop(0, lax.rem(batches, 2), last, 0)

    def turned(lam, carry):
        top = [acc[c, pl.ds(lam, half_tiles, stride=PITCH), :] for c in range(2 * m_parts)]
        low = [acc[c, pl.ds(SUB + lam, half_tiles, stride=PITCH), :] for c in range(2 * m_parts)]
        re = [top[c] - low[m_parts + c] for c in range(m_parts)]
        im = [top[m_parts + c] + low[c] for c in range(m_parts)]
        if width < LANES:
            re = [re[0][:, :width], re[0][:, width:]]
            im = [im[0][:, :width], im[0][:, width:]]
        whole = [jnp.concatenate(x, axis=0).astype(jnp.bfloat16) for x in zip(re, im)]
        parts = len(whole) // 2
        for c in range(parts):
            keep_ref[c, lam] = whole[c]
            give_ref[c, lam] = whole[parts + c]
        return carry

    lax.fori_loop(0, SUB, turned, 0, unroll=4)


def in_lanes(rows):
    width = rows.shape[1]
    if width < LANES:
        return [jnp.concatenate([rows] * (LANES // width), axis=1)]
    return [rows[:, c : c + LANES] for c in range(0, width, LANES)]


def lane_chunks(width):
    return max(1, width // LANES)


def tail_rows(width, share, place, y_of, table, out_t):
    part, depth, m_first = place

    def step(l0, carry):
        z = jnp.dot(table[l0], y_of(l0), preferred_element_type=jnp.float32)
        l1 = part * share + lax.broadcasted_iota(jnp.int32, (share, width), 0)
        l = l0 + 64 * l1 - G // 2
        m = m_first + lax.broadcasted_iota(jnp.int32, (share, width), 1)
        x = l.astype(jnp.float32) * (1.0 / G)
        y = m.astype(jnp.float32) * (1.0 / G)
        ramp = jnp.bitwise_and(-(G - SUB + 1) * l, 2 * G - 1).astype(jnp.float32) * (0.5 / G)
        sc, ss = cos_sin_turns(depth * (jnp.sqrt(1.0 - y * y - x * x) - 1.0) + ramp)
        for c, rows in enumerate(in_lanes(z[:, :width] * sc - z[:, width:] * ss)):
            out_t[c, pl.ds(l0, share, stride=64), :] = rows
        return carry

    lax.fori_loop(0, 64, step, 0, unroll=4)


def turn_out(out_t, out_ref):
    chunk = 128

    def step(n, carry):
        at = pl.multiple_of(n * chunk, chunk)
        for c in range(out_t.shape[0]):
            turned = out_t[c, pl.ds(at, chunk), :].T.astype(out_ref.dtype)
            width = min(LANES, out_ref.shape[0])
            out_ref[c * width : (c + 1) * width, pl.ds(at, chunk)] = turned[:width]
        return carry

    lax.fori_loop(0, out_t.shape[1] // chunk, step, 0, unroll=4)


def head_kernel(
    width, share, places, depths, own_ref, came_ref, head_ref, table, y_ref, out_ref, mid, out_t
):
    def head(lam, carry):
        rhs = jnp.concatenate([own_ref[0, lam], came_ref[0, lam]], axis=0)
        got = jnp.dot(head_ref[...], rhs, preferred_element_type=jnp.float32)
        for c, rows in enumerate(in_lanes(got)):
            mid[c, pl.ds(lam * PITCH, 128), :] = rows
        return carry

    lax.fori_loop(0, SUB, head, 0, unroll=4)

    def y_of(l0):
        halves = []
        for first in (0, 64):
            rows = [mid[c, pl.ds(first + l0, SUB, stride=PITCH), :] for c in range(mid.shape[0])]
            halves += [r[:, : min(width, LANES)] for r in rows]
        y = jnp.concatenate(halves, axis=1).astype(jnp.bfloat16)
        y_ref[l0] = y
        return y

    tail_rows(width, share, (places[0], depths[0], places[1]), y_of, table, out_t)
    turn_out(out_t, out_ref)


def tail_kernel(width, share, places, depths, y_ref, table, out_ref, out_t):
    tail_rows(
        width, share, (places[0], depths[0], places[1]), lambda l0: y_ref[l0], table, out_t
    )
    turn_out(out_t, out_ref)


def finish_kernel(
    width, places, depths, keep_ref, give_ref, head_all, table,
    out_ref, came, mid, y_buf, away, other, out_t, core_send, core_recv, far_send, far_recv,
):
    uv = lax.axis_index("uv")
    wa = lax.axis_index("wa")
    near = {"uv": uv + 1 - 2 * lax.rem(uv, 2)}
    far = {"wa": 1 - wa}
    mesh_type = pl.DeviceIdType.MESH
    barrier = pltpu.get_barrier_semaphore()
    pl.semaphore_signal(barrier, inc=1, device_id=near, device_id_type=mesh_type)
    pl.semaphore_signal(barrier, inc=1, device_id=far, device_id_type=mesh_type)
    pl.semaphore_wait(barrier, 2)

    parts = width // LANES
    lam_step = SUB // SWAPS
    swaps = []
    for c in range(parts):
        for k in range(SWAPS):
            at = pl.ds(k * lam_step, lam_step)
            n = c * SWAPS + k
            swaps.append(
                pltpu.make_async_remote_copy(
                    src_ref=give_ref.at[c, at],
                    dst_ref=came.at[c, at],
                    send_sem=core_send.at[n],
                    recv_sem=core_recv.at[n],
                    device_id=near,
                    device_id_type=mesh_type,
                )
            )
            swaps[-1].start()
    core = lax.rem(uv, 2)

    share = SUB // 2
    step = 64 // SENDS

    def screened(c, l0, part, z):
        l1 = part * share + lax.broadcasted_iota(jnp.int32, (share, LANES), 0)
        l = l0 + 64 * l1 - G // 2
        m = places[1] + c * LANES + lax.broadcasted_iota(jnp.int32, (share, LANES), 1)
        x = l.astype(jnp.float32) * (1.0 / G)
        y = m.astype(jnp.float32) * (1.0 / G)
        ramp = jnp.bitwise_and(-(G - SUB + 1) * l, 2 * G - 1).astype(jnp.float32) * (0.5 / G)
        sc, ss = cos_sin_turns(depths[0] * (jnp.sqrt(1.0 - y * y - x * x) - 1.0) + ramp)
        return z[:, :LANES] * sc - z[:, LANES:] * ss

    sends = []
    for c in range(parts):

        def head(lam, carry, c=c):
            rhs = jnp.concatenate([keep_ref[c, lam], came[c, lam]], axis=0)
            mid[c, pl.ds(lam * PITCH, 128), :] = jnp.dot(
                head_all[core], rhs, preferred_element_type=jnp.float32
            )
            return carry

        for k in range(SWAPS):
            swaps[c * SWAPS + k].wait_recv()
            lax.fori_loop(k * lam_step, (k + 1) * lam_step, head, 0, unroll=4)

        def away_rows(l0, carry, c=c):
            y = jnp.concatenate(
                [mid[c, pl.ds(first + l0, SUB, stride=PITCH), :] for first in (0, 64)], axis=1
            ).astype(jnp.bfloat16)
            y_buf[c, l0] = y
            z = jnp.dot(table[1 - wa, l0], y, preferred_element_type=jnp.float32)
            away[c, l0] = screened(c, l0, 1 - places[0], z).astype(jnp.bfloat16)
            return carry

        for k in range(SENDS):
            lax.fori_loop(k * step, (k + 1) * step, away_rows, 0, unroll=4)
            at = pl.ds(k * step, step)
            n = c * SENDS + k
            sends.append(
                pltpu.make_async_remote_copy(
                    src_ref=away.at[c, at],
                    dst_ref=other.at[c, at],
                    send_sem=far_send.at[n],
                    recv_sem=far_recv.at[n],
                    device_id=far,
                    device_id_type=mesh_type,
                )
            )
            sends[-1].start()

    for c in range(parts):

        def own_rows(l0, carry, c=c):
            z = jnp.dot(table[wa, l0], y_buf[c, l0], preferred_element_type=jnp.float32)
            out_t[c, pl.ds(l0, share, stride=OUT_PITCH), :] = screened(c, l0, places[0], z)
            return carry

        lax.fori_loop(0, 64, own_rows, 0, unroll=4)

    for c in range(parts):

        def add_rows(l0, carry, c=c):
            at = pl.ds(l0, share, stride=OUT_PITCH)
            out_t[c, at, :] += other[c, l0].astype(jnp.float32)
            return carry

        for k in range(SENDS):
            sends[c * SENDS + k].wait_recv()
            lax.fori_loop(k * step, (k + 1) * step, add_rows, 0, unroll=4)

        for n in range(share // 2):
            rows = [out_t[c, pl.ds((2 * n + h) * OUT_PITCH, 64), :] for h in range(2)]
            out_ref[c * LANES : (c + 1) * LANES, n * LANES : (n + 1) * LANES] = jnp.concatenate(
                rows, axis=0
            ).T
    for one in swaps + sends:
        one.wait_send()


def on_device(visibility, coords, tile_row, col_offset, live_count):
    uv_count = lax.axis_size("uv")
    wa_count = lax.axis_size("wa")
    uv_index = lax.axis_index("uv")
    wa_index = lax.axis_index("wa")
    blocks = visibility.shape[0]
    k_len = visibility.shape[2]
    width = G // uv_count
    core = jnp.mod(uv_index, 2)
    partner = uv_index + 1 - 2 * core
    m_first = uv_index * width - G // 2
    m_both = jnp.concatenate(
        [m_first + jnp.arange(width), partner * width + jnp.arange(width) - G // 2]
    )[None, :].astype(jnp.float32) * (0.5 / G)
    numbers = jnp.stack(
        [
            tile_row[:, 0],
            col_offset // SUB,
            jnp.mod(col_offset, SUB),
            jnp.broadcast_to(live_count[0], (blocks,)),
        ]
    )
    numbers = jnp.pad(numbers, ((0, 0), (0, k_len - blocks))).astype(jnp.bfloat16)
    packed = jnp.concatenate([visibility, coords, numbers.reshape(2, 2, k_len)], axis=0)
    all_data = gather_all(packed, uv_count)
    numbers = all_data[:, 2 * blocks :, :, :blocks].reshape(uv_count, 4, blocks)
    numbers = numbers.astype(jnp.int32)
    tiles = numbers[:, 0]
    cols = numbers[:, 1] * SUB + numbers[:, 2]
    cols = jnp.pad(cols, ((0, 0), (0, blocks + 2))).reshape(-1)
    live = jnp.arange(blocks)[None, :] < numbers[:, 3]
    mine = live & (jnp.mod(tiles, 2) == core)
    homes = jnp.where(mine, tiles // 2, G // SUB // 2).reshape(-1)
    half_tiles = G // SUB // 2
    cap = 2 * uv_count
    shape = (lane_chunks(width), SUB, SUB, min(width, LANES))
    vmem = pl.BlockSpec(memory_space=pltpu.VMEM)
    smem = pl.BlockSpec(memory_space=pltpu.SMEM)
    m_parts = 2 * width // LANES
    k_parts = k_len // LANES
    buffers = [
        pltpu.VMEM((2, 2, k_parts, 72, LANES), jnp.float32),
        pltpu.VMEM((8, k_parts, BATCH, LANES), jnp.float32),
        pltpu.VMEM((3, k_parts, BATCH, LANES), jnp.float32),
        pltpu.VMEM((3, m_parts, BATCH, LANES), jnp.float32),
    ]
    own, give = pl.pallas_call(
        functools.partial(grid_kernel, width, blocks),
        out_shape=[jax.ShapeDtypeStruct(shape, jnp.bfloat16)] * 2,
        in_specs=[smem, smem, smem, vmem, vmem, vmem],
        out_specs=[vmem, vmem],
        scratch_shapes=[
            pltpu.VMEM((2 * m_parts, half_tiles * PITCH, LANES), jnp.float32),
            pltpu.SMEM((half_tiles * cap + uv_count * blocks,), jnp.int32),
            pltpu.SMEM((half_tiles + 1,), jnp.int32),
            pltpu.SMEM((3 * (uv_count * blocks // STACK + half_tiles),), jnp.int32),
            pltpu.SMEM((3 * (half_tiles + 1),), jnp.int32),
            pltpu.VMEM((SUB, 2 * width), jnp.float32),
            pltpu.VMEM((5, k_parts, BATCH, LANES), jnp.float32),
        ]
        + buffers
        + buffers,
        compiler_params=pltpu.CompilerParams(vmem_limit_bytes=32 * 1024 * 1024),
    )(
        homes,
        cols,
        numbers[:, 3, 0],
        all_data.reshape((-1,) + all_data.shape[2:]),
        m_both,
        jnp.asarray(column_table(uv_count)),
    )
    share = 64 // wa_count
    depth = ((wa_index.astype(jnp.float32) - (wa_count - 1) / 2.0) * plane_step)[None]
    tables = jnp.asarray(row_table(wa_count))
    span = G // wa_count

    def places_of(part):
        return jnp.stack([part, m_first]).astype(jnp.int32)

    def head_of(part, dtype):
        return pl.pallas_call(
            functools.partial(head_kernel, width, share),
            out_shape=[
                jax.ShapeDtypeStruct((64, SUB, 2 * width), jnp.bfloat16),
                jax.ShapeDtypeStruct((width, span), dtype),
            ],
            in_specs=[smem, smem, vmem, vmem, vmem, vmem],
            out_specs=[vmem, vmem],
            scratch_shapes=[
                pltpu.VMEM((lane_chunks(width), SUB * PITCH, LANES), jnp.float32),
                pltpu.VMEM((lane_chunks(width), span, LANES), jnp.float32),
            ],
            compiler_params=pltpu.CompilerParams(vmem_limit_bytes=40 * 1024 * 1024),
        )(
            places_of(part), depth, own, came_half, jnp.asarray(head_matrices())[core], tables[part]
        )

    def tail_of(part, first, dtype):
        return pl.pallas_call(
            functools.partial(tail_kernel, width, share),
            out_shape=jax.ShapeDtypeStruct((width, span), dtype),
            in_specs=[smem, smem, vmem, vmem],
            out_specs=vmem,
            scratch_shapes=[pltpu.VMEM((lane_chunks(width), span, LANES), jnp.float32)],
            compiler_params=pltpu.CompilerParams(vmem_limit_bytes=40 * 1024 * 1024),
        )(places_of(part), depth, first, tables[part])

    if wa_count == 2 and width % LANES == 0:
        parts = width // LANES
        scratch = [
            pltpu.VMEM(shape, jnp.bfloat16),
            pltpu.VMEM((parts, SUB * PITCH, LANES), jnp.float32),
            pltpu.VMEM((parts, 64, SUB, 2 * LANES), jnp.bfloat16),
            pltpu.VMEM((parts, 64, share, LANES), jnp.bfloat16),
            pltpu.VMEM((parts, 64, share, LANES), jnp.bfloat16),
            pltpu.VMEM((parts, share * OUT_PITCH, LANES), jnp.float32),
        ]
        scratch += [pltpu.SemaphoreType.DMA((parts * SWAPS,))] * 2
        scratch += [pltpu.SemaphoreType.DMA((parts * SENDS,))] * 2
        return pl.pallas_call(
            functools.partial(finish_kernel, width),
            out_shape=jax.ShapeDtypeStruct((width, span), jnp.float32),
            in_specs=[smem, smem] + [vmem] * 4,
            out_specs=vmem,
            scratch_shapes=scratch,
            compiler_params=pltpu.CompilerParams(
                collective_id=1, has_side_effects=True, vmem_limit_bytes=24 * 1024 * 1024
            ),
        )(
            places_of(wa_index),
            depth,
            own,
            give,
            jnp.asarray(head_matrices()),
            tables,
        )
    came_half = lax.ppermute(give, "uv", [(n, n ^ 1) for n in range(uv_count)])

    first, part = head_of(jnp.int32(0), jnp.bfloat16)
    images = [part] + [tail_of(jnp.int32(n), first, jnp.bfloat16) for n in range(1, wa_count)]
    parts = jnp.stack(images, axis=1)
    came = lax.all_to_all(parts, "wa", split_axis=1, concat_axis=1)
    return jnp.sum(came.astype(jnp.float32), axis=1)


def solution(mesh):
    in_specs = (
        P(("wa", "uv"), None, None),
        P(("wa", "uv"), None, None),
        P(("wa", "uv"), None),
        P(("wa", "uv")),
        P("wa", "uv"),
    )
    return jax.shard_map(
        on_device, mesh=mesh, in_specs=in_specs, out_specs=P("uv", "wa"), check_vma=False
    )
```

```python
import functools
import math

import jax
import jax.numpy as jnp
import ml_dtypes
import numpy as np
from jax import lax
from jax.experimental import pallas as pl
from jax.experimental.pallas import tpu as pltpu
from jax.sharding import PartitionSpec as P

G = 4096
SUB = 64
BATCH = 8
PLACES = 8
WIPE = 72
STACK = 4
LANES = 128
PITCH = 129
OUT_PITCH = 65
SWAPS = 2
SENDS = 4
plane_step = 6.0
full_turn = 2.0 * math.pi
BF = ml_dtypes.bfloat16


def turn_poly(bound, degree):
    nodes = np.cos(np.pi * (np.arange(256) + 0.5) / 256)
    z = (nodes + 1.0) / (2.0 * bound)
    f = np.sqrt(z)
    cos_c = np.polynomial.chebyshev.cheb2poly(
        np.polynomial.chebyshev.chebfit(nodes, np.cos(2 * np.pi * f), degree)
    )
    sin_c = np.polynomial.chebyshev.cheb2poly(
        np.polynomial.chebyshev.chebfit(nodes, np.sin(2 * np.pi * f) / f, degree)
    )
    base = np.polynomial.Polynomial([-1.0, 2.0 * bound])
    out = []
    for coefs in (cos_c, sin_c):
        total = np.polynomial.Polynomial([0.0])
        for c in coefs[::-1]:
            total = total * base + c
        out.append([float(c) for c in total.coef])
    return out


COS_C, SIN_C = turn_poly(4.0, 5)
COS_S, SIN_S = turn_poly(16.0, 4)


def cos_sin_part(f, cos_c, sin_c):
    z = f * f
    c = cos_c[-1] * z + cos_c[-2]
    for k in cos_c[-3::-1]:
        c = c * z + k
    s = sin_c[-1] * z + sin_c[-2]
    for k in sin_c[-3::-1]:
        s = s * z + k
    return c, s * f


def cos_sin_turns(turns):
    return cos_sin_part(turns - jnp.round(turns), COS_C, SIN_C)


def times(a, b):
    return a[0] * b[0] - a[1] * b[1], a[0] * b[1] + a[1] * b[0]


def squared(a):
    twice = a[0] + a[0]
    return twice * a[0] - 1.0, twice * a[1]


def half_orders():
    fine = np.arange(8) + 0.5
    return np.concatenate([fine, 16 - fine, 16 + fine, 32 - fine])


def dirichlet(x):
    bottom = np.sin(np.pi * x / SUB)
    zero = np.abs(bottom) < 1e-12
    return np.where(zero, float(SUB), np.sin(np.pi * x) / np.where(zero, 1.0, bottom))


def spread_table():
    at = (np.arange(G) - G // 2) / SUB + 0.5
    order = half_orders()[:, None]
    minus, plus = dirichlet(at[None] - order), dirichlet(at[None] + order)
    return np.concatenate([minus + plus, minus - plus], axis=0)


def column_table(devices):
    whole = (spread_table() / SUB).reshape(SUB, devices, G // devices)
    return np.ascontiguousarray(whole.transpose(1, 0, 2)).astype(np.float32)


def row_table(parts):
    whole = (spread_table() / G).reshape(SUB, parts, SUB // parts, 64)
    return np.ascontiguousarray(whole.transpose(1, 3, 2, 0)).astype(BF)


def head_matrices():
    l0 = np.arange(64)[:, None]
    out = []
    for core in range(2):
        columns = []
        for source in range(2):
            t = (2 * np.arange(32) + (core ^ source))[None, :]
            ang = full_turn / 64 * np.mod(l0 * t, 64)
            c, s = np.cos(ang), np.sin(ang)
            columns.append(np.block([[c, -s], [s, c]]))
        out.append(np.concatenate(columns, axis=1))
    return np.stack(out).astype(BF)


def gather_kernel(
    far, near, x_ref, out_ref,
    own_sem, ring_send, ring_recv, side_send, side_recv, core_send, core_recv,
):
    uv = lax.axis_index("uv")
    c = lax.rem(uv, 2)
    b = lax.rem(uv // 2, near)
    a = uv // (2 * near)
    mesh_type = pl.DeviceIdType.MESH
    sources = (x_ref,)
    outs = (out_ref,)

    def at(da, db, dc):
        return ((a + da) * near + lax.rem(b + db + near, near)) * 2 + lax.rem(c + dc, 2)

    def inside(da):
        return jnp.logical_and(a + da >= 0, a + da < far)

    barrier = pltpu.get_barrier_semaphore()

    def greet(device):
        pl.semaphore_signal(barrier, inc=1, device_id={"uv": device}, device_id_type=mesh_type)

    for side in (-1, 1):
        pl.when(inside(side))(lambda side=side: greet(at(side, 0, 0)))
    for e in range(1, near):
        greet(at(0, e, 0))
    greet(at(0, 0, 1))
    mine = [
        pltpu.make_async_copy(sources[k], outs[k].at[uv], own_sem.at[k]) for k in range(1)
    ]
    for one in mine:
        one.start()
    beside = jnp.where(a > 0, 1, 0) + jnp.where(a < far - 1, 1, 0)
    pl.semaphore_wait(barrier, beside + near)

    def copy(k, own, slot, target, send, recv):
        return pltpu.make_async_remote_copy(
            src_ref=sources[k] if own else outs[k].at[slot],
            dst_ref=outs[k].at[slot],
            send_sem=send,
            recv_sem=recv,
            device_id={"uv": target},
            device_id_type=mesh_type,
        )

    first = (0,)
    second = ()
    sends = []

    def start(valid, one):
        pl.when(valid)(lambda: one.start())
        sends.append((valid, one))

    def along(k, da, e, own):
        slot = at(da, -e, 0)
        if da <= 0:
            n = (k * near + e) * 2 * far - da
            start(
                jnp.logical_and(inside(da), inside(1)),
                copy(k, own, slot, at(1, 0, 0), ring_send.at[n], ring_recv.at[n + 1]),
            )
        if da >= 0:
            n = ((k * near + e) * 2 + 1) * far + da
            start(
                jnp.logical_and(inside(da), inside(-1)),
                copy(k, own, slot, at(-1, 0, 0), ring_send.at[n], ring_recv.at[n + 1]),
            )

    def arrived_along(k, da, e):
        slot = at(da, -e, 0)
        n = (k * near + e) * 2 * far - da if da < 0 else ((k * near + e) * 2 + 1) * far + da
        one = copy(k, False, slot, uv ^ 1, ring_send.at[n], ring_recv.at[n])
        pl.when(inside(da))(lambda: one.wait_recv())

    def aside(k, da, own):
        for e in range(1, near):
            n = (k * (2 * far) + far + da) * near + e
            start(
                inside(da),
                copy(k, own, at(da, 0, 0), at(0, e, 0), side_send.at[n], side_recv.at[n]),
            )

    def arrived_aside(k, da, e):
        n = (k * (2 * far) + far + da) * near + e
        one = copy(k, False, at(da, -e, 0), uv ^ 1, side_send.at[n], side_recv.at[n])
        pl.when(inside(da))(lambda: one.wait_recv())

    def across(k, da, e, own):
        n = (k * (2 * far) + far + da) * near + e
        start(
            inside(da),
            copy(k, own, at(da, -e, 0), at(0, 0, 1), core_send.at[n], core_recv.at[n]),
        )

    for k in second:
        aside(k, 0, True)
    for k in first:
        along(k, 0, 0, True)
    for k in second:
        along(k, 0, 0, True)
    for k in first:
        aside(k, 0, True)
    for k in range(1):
        across(k, 0, 0, True)
    for e in range(1, near):
        for k in second:
            arrived_aside(k, 0, e)
            along(k, 0, e, False)
            across(k, 0, e, False)
    for s in range(1, far):
        for k in first:
            for da in (-s, s):
                arrived_along(k, da, 0)
                along(k, da, 0, False)
                aside(k, da, False)
                across(k, da, 0, False)
        for e in range(near):
            for k in second:
                for da in (-s, s):
                    arrived_along(k, da, e)
                    along(k, da, e, False)
                    across(k, da, e, False)
    for k in first:
        for da in sorted(range(1 - far, far), key=abs):
            for e in range(1, near):
                arrived_aside(k, da, e)
                across(k, da, e, False)
    for da in sorted(range(1 - far, far), key=abs):
        for e in range(near):
            for k in range(1):
                n = (k * (2 * far) + far + da) * near + e
                one = copy(k, False, at(da, -e, 1), uv ^ 1, core_send.at[n], core_recv.at[n])
                pl.when(inside(da))(lambda one=one: one.wait_recv())
    for one in mine:
        one.wait()
    for valid, one in sends:
        pl.when(valid)(lambda one=one: one.wait_send())


def gather_all(packed, uv_count):
    chips = uv_count // 2
    near = 1 << ((chips.bit_length() - 1) // 2)
    far = chips // near
    sems = [1] + [near * 2 * far + 1] * 2 + [2 * far * near] * 4
    return pl.pallas_call(
        functools.partial(gather_kernel, far, near),
        out_shape=jax.ShapeDtypeStruct((uv_count,) + packed.shape, packed.dtype),
        in_specs=[pl.BlockSpec(memory_space=pltpu.VMEM)],
        out_specs=pl.BlockSpec(memory_space=pltpu.VMEM),
        scratch_shapes=[pltpu.SemaphoreType.DMA((n,)) for n in sems],
        compiler_params=pltpu.CompilerParams(
            collective_id=0, has_side_effects=True, vmem_limit_bytes=16 * 1024 * 1024
        ),
    )(packed)


def grid_kernel(
    width, blocks, homes, cols, counts, data_ref, m_ref, d_all, keep_ref, give_ref,
    acc, slots, filled, fours, twos, d_ref, *buffers,
):
    each = 2 * blocks + 2
    devices = data_ref.shape[0] // each
    k_len = data_ref.shape[2]
    cap = 2 * devices
    half_tiles = G // SUB // 2
    both = 2 * width
    k_parts = k_len // LANES
    m_parts = both // LANES
    uv = lax.axis_index("uv")
    stage = buffers[0]
    sets = (buffers[1:5], buffers[5:9])
    d_ref[:, :width] = d_all[uv]
    d_ref[:, width:] = d_all[uv + 1 - 2 * lax.rem(uv, 2)]

    for n in range(3):
        fours[n] = 0
        twos[n] = 0

    def empty(h, carry):
        filled[h] = 0
        return carry

    lax.fori_loop(0, half_tiles + 1, empty, 0)
    wipes = acc.shape[1] // WIPE

    def wipe(n):
        at = pl.multiple_of(jnp.minimum(n, wipes - 1) * WIPE, WIPE)
        for c in range(2 * m_parts):
            acc[c, pl.ds(at, WIPE), :] = jnp.zeros((WIPE, LANES), jnp.float32)


    def spread(j, carry):
        def place(n, inner):
            wipe(inner)
            for k in range(PLACES):
                i = n * PLACES + k
                h = homes[j * blocks + i]
                n_h = filled[h]
                slots[h * cap + n_h] = j * each + i
                filled[h] = n_h + 1
            return inner + 1

        return lax.fori_loop(0, (counts[j] + PLACES - 1) // PLACES, place, carry)

    def wipe_rest(n, carry):
        wipe(n)
        return carry

    lax.fori_loop(lax.fori_loop(0, devices, spread, 0), wipes, wipe_rest, 0)

    def list_groups(h, found):
        count = filled[h]
        whole = (count + 1) // STACK

        def one(g, n):
            fours[3 * n] = h
            fours[3 * n + 1] = h * cap + STACK * g
            fours[3 * n + 2] = count - STACK * g
            return n + 1

        n, m = found
        n = lax.fori_loop(0, whole, one, n)
        rest = count - STACK * whole
        twos[3 * m] = h
        twos[3 * m + 1] = h * cap + STACK * whole
        twos[3 * m + 2] = rest
        return n, m + jnp.where(rest > 0, 1, 0)

    n_fours, n_twos = lax.fori_loop(0, half_tiles, list_groups, (0, 0))
    scale = 1.0 / math.sqrt(k_len)

    def prepare(batch, refs, stack, group, total):
        fine, coarse, signal, phase = refs
        for p in range(BATCH // stack):
            n = batch * (BATCH // stack) + p
            real = n < total
            n = jnp.where(real, n, 0)
            first = group[3 * n + 1]
            left_over = jnp.where(real, group[3 * n + 2], 0)
            for q in range(stack):
                live = q < left_over
                row = jnp.where(live, slots[first + q], 0)
                centre = (2 * cols[row] - (G - SUB + 1)).astype(jnp.float32)
                keep = jnp.where(live, scale, 0.0)
                k = p * stack + q
                signals = data_ref[row].astype(jnp.float32) * keep
                places = data_ref[row + blocks].astype(jnp.float32)
                for c in range(k_parts):
                    cut = slice(c * LANES, (c + 1) * LANES)
                    for r in range(2):
                        stage[r, c, k : k + 1, :] = signals[r : r + 1, cut]
                        stage[2 + r, c, k : k + 1, :] = places[r : r + 1, cut]
                stage[4, 0, k : k + 1, :] = jnp.full((1, LANES), centre, jnp.float32)
        for c in range(k_parts):
            halves = []
            for axis in range(2):
                turns = (stage[2 + axis, c] + 0.5) * (0.5 / SUB)
                half = cos_sin_part(turns, COS_S, SIN_S)
                halves.append(half)
                step = squared(half)
                power = half
                for b in range(8):
                    if b:
                        power = times(power, step)
                    for e in range(2):
                        fine[axis, e, c, b * 9 : b * 9 + 8, :] = power[e]
                power = squared(times(power, half))
                for e in range(2):
                    coarse[4 * axis + e, c] = power[e]
                power = squared(power)
                for e in range(2):
                    coarse[4 * axis + 2 + e, c] = power[e]
            hc, hs = times(*halves)
            vr, vi = stage[0, c], stage[1, c]
            signal[0, c] = vr * hc + vi * hs
            wi = vi * hc - vr * hs
            signal[1, c] = wi
            signal[2, c] = -wi
        for c in range(m_parts):
            pc, ps = cos_sin_turns(stage[4, 0] * m_ref[:, c * LANES : (c + 1) * LANES])
            phase[0, c] = pc
            phase[1, c] = ps
            phase[2, c] = -ps

    def expand(c, s, c1, s1, c2, s2):
        a, b, d, e = c1 * c, s1 * s, s1 * c, c1 * s
        return (
            jnp.concatenate([c, a + b, a - b, c2 * c + s2 * s], axis=0),
            jnp.concatenate([s, d - e, d + e, s2 * c - c2 * s], axis=0),
        )

    def piece_of(k, refs):
        fine, coarse, signal, _ = refs
        lefts, rights = [], []
        for c in range(k_parts):
            tables = []
            for axis in range(2):
                start = [fine[axis, e, c, pl.ds(k, 8, stride=9), :] for e in range(2)]
                rows = [coarse[4 * axis + n, c, k : k + 1, :] for n in range(4)]
                tables.append(expand(*start, *rows))
            (cu, su), (cv, sv) = tables
            wr, wi, nwi = (signal[n, c, k : k + 1, :] for n in range(3))
            lefts.append(
                jnp.concatenate([wr * cu, nwi * su, wi * cu, wr * su], axis=0).astype(jnp.bfloat16)
            )
            rights.append(jnp.concatenate([cv, sv], axis=0).astype(jnp.bfloat16))
        return lax.dot_general(
            jnp.concatenate(lefts, axis=1),
            jnp.concatenate(rights, axis=1),
            (((1,), (1,)), ((), ())),
            preferred_element_type=jnp.float32,
        ).astype(jnp.bfloat16)

    def gather_up(batch, refs, stack, group, total):
        phase = refs[3]
        pieces = [
            jnp.concatenate([piece_of(k, refs) for k in range(p * stack, (p + 1) * stack)], axis=1)
            for p in range(BATCH // stack)
        ]
        for p in range(BATCH // stack):
            n = batch * (BATCH // stack) + p
            h = group[3 * jnp.where(n < total, n, 0)]
            rows = pl.ds(h * PITCH, 2 * SUB)
            ks = range(p * stack, (p + 1) * stack)
            piece = pieces[p]
            wide = min(2, m_parts)
            for c0 in range(0, m_parts, wide):
                tops = [d_ref[:32, c * LANES : (c + 1) * LANES] for c in range(c0, c0 + wide)]
                lows = [d_ref[32:, c * LANES : (c + 1) * LANES] for c in range(c0, c0 + wide)]
                for turn in range(2):
                    weight = []
                    for k in ks:
                        top, low = [], []
                        for c in range(c0, c0 + wide):
                            pr, pi, npi = (phase[e, c, k : k + 1, :] for e in range(3))
                            top.append(tops[c - c0] * (pi if turn else pr))
                            low.append(lows[c - c0] * (pr if turn else npi))
                        weight += [jnp.concatenate(top, axis=1), jnp.concatenate(low, axis=1)]
                    got = jnp.dot(
                        piece,
                        jnp.concatenate(weight, axis=0).astype(jnp.bfloat16),
                        preferred_element_type=jnp.float32,
                    )
                    for c in range(wide):
                        at = turn * m_parts + c0 + c
                        acc[at, rows, :] += got[:, c * LANES : (c + 1) * LANES]

    for stack, group, total in ((STACK, fours, n_fours), (2, twos, n_twos)):
        batches = (total + BATCH // stack - 1) // (BATCH // stack)
        rest = (stack, group, total)
        prepare(0, sets[0], *rest)

        def step(it, carry, rest=rest):
            for n in range(2):
                gather_up(2 * it + n, sets[n], *rest)
                prepare(2 * it + n + 1, sets[1 - n], *rest)
            return carry

        lax.fori_loop(0, batches // 2, step, 0)

        def last(it, carry, rest=rest, batches=batches):
            gather_up(batches - 1, sets[0], *rest)
            return carry

        lax.fori_loop(0, lax.rem(batches, 2), last, 0)

    def turned(lam, carry):
        top = [acc[c, pl.ds(lam, half_tiles, stride=PITCH), :] for c in range(2 * m_parts)]
        low = [acc[c, pl.ds(SUB + lam, half_tiles, stride=PITCH), :] for c in range(2 * m_parts)]
        re = [top[c] - low[m_parts + c] for c in range(m_parts)]
        im = [top[m_parts + c] + low[c] for c in range(m_parts)]
        if width < LANES:
            re = [re[0][:, :width], re[0][:, width:]]
            im = [im[0][:, :width], im[0][:, width:]]
        whole = [jnp.concatenate(x, axis=0).astype(jnp.bfloat16) for x in zip(re, im)]
        parts = len(whole) // 2
        for c in range(parts):
            keep_ref[c, lam] = whole[c]
            give_ref[c, lam] = whole[parts + c]
        return carry

    lax.fori_loop(0, SUB, turned, 0, unroll=4)


def in_lanes(rows):
    width = rows.shape[1]
    if width < LANES:
        return [jnp.concatenate([rows] * (LANES // width), axis=1)]
    return [rows[:, c : c + LANES] for c in range(0, width, LANES)]


def lane_chunks(width):
    return max(1, width // LANES)


def tail_rows(width, share, place, y_of, table, out_t):
    part, depth, m_first = place

    def step(l0, carry):
        z = jnp.dot(table[l0], y_of(l0), preferred_element_type=jnp.float32)
        l1 = part * share + lax.broadcasted_iota(jnp.int32, (share, width), 0)
        l = l0 + 64 * l1 - G // 2
        m = m_first + lax.broadcasted_iota(jnp.int32, (share, width), 1)
        x = l.astype(jnp.float32) * (1.0 / G)
        y = m.astype(jnp.float32) * (1.0 / G)
        ramp = jnp.bitwise_and(-(G - SUB + 1) * l, 2 * G - 1).astype(jnp.float32) * (0.5 / G)
        sc, ss = cos_sin_turns(depth * (jnp.sqrt(1.0 - y * y - x * x) - 1.0) + ramp)
        for c, rows in enumerate(in_lanes(z[:, :width] * sc - z[:, width:] * ss)):
            out_t[c, pl.ds(l0, share, stride=64), :] = rows
        return carry

    lax.fori_loop(0, 64, step, 0, unroll=4)


def turn_out(out_t, out_ref):
    chunk = 128

    def step(n, carry):
        at = pl.multiple_of(n * chunk, chunk)
        for c in range(out_t.shape[0]):
            turned = out_t[c, pl.ds(at, chunk), :].T.astype(out_ref.dtype)
            width = min(LANES, out_ref.shape[0])
            out_ref[c * width : (c + 1) * width, pl.ds(at, chunk)] = turned[:width]
        return carry

    lax.fori_loop(0, out_t.shape[1] // chunk, step, 0, unroll=4)


def head_kernel(
    width, share, places, depths, own_ref, came_ref, head_ref, table, y_ref, out_ref, mid, out_t
):
    def head(lam, carry):
        rhs = jnp.concatenate([own_ref[0, lam], came_ref[0, lam]], axis=0)
        got = jnp.dot(head_ref[...], rhs, preferred_element_type=jnp.float32)
        for c, rows in enumerate(in_lanes(got)):
            mid[c, pl.ds(lam * PITCH, 128), :] = rows
        return carry

    lax.fori_loop(0, SUB, head, 0, unroll=4)

    def y_of(l0):
        halves = []
        for first in (0, 64):
            rows = [mid[c, pl.ds(first + l0, SUB, stride=PITCH), :] for c in range(mid.shape[0])]
            halves += [r[:, : min(width, LANES)] for r in rows]
        y = jnp.concatenate(halves, axis=1).astype(jnp.bfloat16)
        y_ref[l0] = y
        return y

    tail_rows(width, share, (places[0], depths[0], places[1]), y_of, table, out_t)
    turn_out(out_t, out_ref)


def tail_kernel(width, share, places, depths, y_ref, table, out_ref, out_t):
    tail_rows(
        width, share, (places[0], depths[0], places[1]), lambda l0: y_ref[l0], table, out_t
    )
    turn_out(out_t, out_ref)


def finish_kernel(
    width, places, depths, keep_ref, give_ref, head_all, table,
    out_ref, came, mid, y_buf, away, other, out_t, core_send, core_recv, far_send, far_recv,
):
    uv = lax.axis_index("uv")
    wa = lax.axis_index("wa")
    near = {"uv": uv + 1 - 2 * lax.rem(uv, 2)}
    far = {"wa": 1 - wa}
    mesh_type = pl.DeviceIdType.MESH
    barrier = pltpu.get_barrier_semaphore()
    pl.semaphore_signal(barrier, inc=1, device_id=near, device_id_type=mesh_type)
    pl.semaphore_signal(barrier, inc=1, device_id=far, device_id_type=mesh_type)
    pl.semaphore_wait(barrier, 2)

    parts = width // LANES
    lam_step = SUB // SWAPS
    swaps = []
    for c in range(parts):
        for k in range(SWAPS):
            at = pl.ds(k * lam_step, lam_step)
            n = c * SWAPS + k
            swaps.append(
                pltpu.make_async_remote_copy(
                    src_ref=give_ref.at[c, at],
                    dst_ref=came.at[c, at],
                    send_sem=core_send.at[n],
                    recv_sem=core_recv.at[n],
                    device_id=near,
                    device_id_type=mesh_type,
                )
            )
            swaps[-1].start()
    core = lax.rem(uv, 2)

    share = SUB // 2
    step = 64 // SENDS

    def screened(c, l0, part, z):
        l1 = part * share + lax.broadcasted_iota(jnp.int32, (share, LANES), 0)
        l = l0 + 64 * l1 - G // 2
        m = places[1] + c * LANES + lax.broadcasted_iota(jnp.int32, (share, LANES), 1)
        x = l.astype(jnp.float32) * (1.0 / G)
        y = m.astype(jnp.float32) * (1.0 / G)
        ramp = jnp.bitwise_and(-(G - SUB + 1) * l, 2 * G - 1).astype(jnp.float32) * (0.5 / G)
        sc, ss = cos_sin_turns(depths[0] * (jnp.sqrt(1.0 - y * y - x * x) - 1.0) + ramp)
        return z[:, :LANES] * sc - z[:, LANES:] * ss

    sends = []
    for c in range(parts):

        def head(lam, carry, c=c):
            rhs = jnp.concatenate([keep_ref[c, lam], came[c, lam]], axis=0)
            mid[c, pl.ds(lam * PITCH, 128), :] = jnp.dot(
                head_all[core], rhs, preferred_element_type=jnp.float32
            )
            return carry

        for k in range(SWAPS):
            swaps[c * SWAPS + k].wait_recv()
            lax.fori_loop(k * lam_step, (k + 1) * lam_step, head, 0, unroll=16)

        def away_rows(l0, carry, c=c):
            y = jnp.concatenate(
                [mid[c, pl.ds(first + l0, SUB, stride=PITCH), :] for first in (0, 64)], axis=1
            ).astype(jnp.bfloat16)
            y_buf[c, l0] = y
            z = jnp.dot(table[1 - wa, l0], y, preferred_element_type=jnp.float32)
            away[c, l0] = screened(c, l0, 1 - places[0], z).astype(jnp.bfloat16)
            return carry

        for k in range(SENDS):
            lax.fori_loop(k * step, (k + 1) * step, away_rows, 0, unroll=16)
            at = pl.ds(k * step, step)
            n = c * SENDS + k
            sends.append(
                pltpu.make_async_remote_copy(
                    src_ref=away.at[c, at],
                    dst_ref=other.at[c, at],
                    send_sem=far_send.at[n],
                    recv_sem=far_recv.at[n],
                    device_id=far,
                    device_id_type=mesh_type,
                )
            )
            sends[-1].start()

    for c in range(parts):

        def own_rows(l0, carry, c=c):
            z = jnp.dot(table[wa, l0], y_buf[c, l0], preferred_element_type=jnp.float32)
            out_t[c, pl.ds(l0, share, stride=OUT_PITCH), :] = screened(c, l0, places[0], z)
            return carry

        lax.fori_loop(0, 64, own_rows, 0, unroll=16)

    for c in range(parts):

        def add_rows(l0, carry, c=c):
            at = pl.ds(l0, share, stride=OUT_PITCH)
            out_t[c, at, :] += other[c, l0].astype(jnp.float32)
            return carry

        for k in range(SENDS):
            sends[c * SENDS + k].wait_recv()
            lax.fori_loop(k * step, (k + 1) * step, add_rows, 0, unroll=16)

        for n in range(share // 2):
            rows = [out_t[c, pl.ds((2 * n + h) * OUT_PITCH, 64), :] for h in range(2)]
            out_ref[c * LANES : (c + 1) * LANES, n * LANES : (n + 1) * LANES] = jnp.concatenate(
                rows, axis=0
            ).T
    for one in swaps + sends:
        one.wait_send()


def on_device(visibility, coords, tile_row, col_offset, live_count):
    uv_count = lax.axis_size("uv")
    wa_count = lax.axis_size("wa")
    uv_index = lax.axis_index("uv")
    wa_index = lax.axis_index("wa")
    blocks = visibility.shape[0]
    k_len = visibility.shape[2]
    width = G // uv_count
    core = jnp.mod(uv_index, 2)
    partner = uv_index + 1 - 2 * core
    m_first = uv_index * width - G // 2
    m_both = jnp.concatenate(
        [m_first + jnp.arange(width), partner * width + jnp.arange(width) - G // 2]
    )[None, :].astype(jnp.float32) * (0.5 / G)
    numbers = jnp.stack(
        [
            tile_row[:, 0],
            col_offset // SUB,
            jnp.mod(col_offset, SUB),
            jnp.broadcast_to(live_count[0], (blocks,)),
        ]
    )
    numbers = jnp.pad(numbers, ((0, 0), (0, k_len - blocks))).astype(jnp.bfloat16)
    packed = jnp.concatenate([visibility, coords, numbers.reshape(2, 2, k_len)], axis=0)
    all_data = gather_all(packed, uv_count)
    numbers = all_data[:, 2 * blocks :, :, :blocks].reshape(uv_count, 4, blocks)
    numbers = numbers.astype(jnp.int32)
    tiles = numbers[:, 0]
    cols = numbers[:, 1] * SUB + numbers[:, 2]
    cols = jnp.pad(cols, ((0, 0), (0, blocks + 2))).reshape(-1)
    live = jnp.arange(blocks)[None, :] < numbers[:, 3]
    mine = live & (jnp.mod(tiles, 2) == core)
    homes = jnp.where(mine, tiles // 2, G // SUB // 2).reshape(-1)
    half_tiles = G // SUB // 2
    cap = 2 * uv_count
    shape = (lane_chunks(width), SUB, SUB, min(width, LANES))
    vmem = pl.BlockSpec(memory_space=pltpu.VMEM)
    smem = pl.BlockSpec(memory_space=pltpu.SMEM)
    m_parts = 2 * width // LANES
    k_parts = k_len // LANES
    buffers = [
        pltpu.VMEM((2, 2, k_parts, 72, LANES), jnp.float32),
        pltpu.VMEM((8, k_parts, BATCH, LANES), jnp.float32),
        pltpu.VMEM((3, k_parts, BATCH, LANES), jnp.float32),
        pltpu.VMEM((3, m_parts, BATCH, LANES), jnp.float32),
    ]
    own, give = pl.pallas_call(
        functools.partial(grid_kernel, width, blocks),
        out_shape=[jax.ShapeDtypeStruct(shape, jnp.bfloat16)] * 2,
        in_specs=[smem, smem, smem, vmem, vmem, vmem],
        out_specs=[vmem, vmem],
        scratch_shapes=[
            pltpu.VMEM((2 * m_parts, -(-half_tiles * PITCH // WIPE) * WIPE, LANES), jnp.float32),
            pltpu.SMEM((half_tiles * cap + uv_count * blocks,), jnp.int32),
            pltpu.SMEM((half_tiles + 1,), jnp.int32),
            pltpu.SMEM((3 * (uv_count * blocks // STACK + half_tiles),), jnp.int32),
            pltpu.SMEM((3 * (half_tiles + 1),), jnp.int32),
            pltpu.VMEM((SUB, 2 * width), jnp.float32),
            pltpu.VMEM((5, k_parts, BATCH, LANES), jnp.float32),
        ]
        + buffers
        + buffers,
        compiler_params=pltpu.CompilerParams(vmem_limit_bytes=32 * 1024 * 1024),
    )(
        homes,
        cols,
        numbers[:, 3, 0],
        all_data.reshape((-1,) + all_data.shape[2:]),
        m_both,
        jnp.asarray(column_table(uv_count)),
    )
    share = 64 // wa_count
    depth = ((wa_index.astype(jnp.float32) - (wa_count - 1) / 2.0) * plane_step)[None]
    tables = jnp.asarray(row_table(wa_count))
    span = G // wa_count

    def places_of(part):
        return jnp.stack([part, m_first]).astype(jnp.int32)

    def head_of(part, dtype):
        return pl.pallas_call(
            functools.partial(head_kernel, width, share),
            out_shape=[
                jax.ShapeDtypeStruct((64, SUB, 2 * width), jnp.bfloat16),
                jax.ShapeDtypeStruct((width, span), dtype),
            ],
            in_specs=[smem, smem, vmem, vmem, vmem, vmem],
            out_specs=[vmem, vmem],
            scratch_shapes=[
                pltpu.VMEM((lane_chunks(width), SUB * PITCH, LANES), jnp.float32),
                pltpu.VMEM((lane_chunks(width), span, LANES), jnp.float32),
            ],
            compiler_params=pltpu.CompilerParams(vmem_limit_bytes=40 * 1024 * 1024),
        )(
            places_of(part), depth, own, came_half, jnp.asarray(head_matrices())[core], tables[part]
        )

    def tail_of(part, first, dtype):
        return pl.pallas_call(
            functools.partial(tail_kernel, width, share),
            out_shape=jax.ShapeDtypeStruct((width, span), dtype),
            in_specs=[smem, smem, vmem, vmem],
            out_specs=vmem,
            scratch_shapes=[pltpu.VMEM((lane_chunks(width), span, LANES), jnp.float32)],
            compiler_params=pltpu.CompilerParams(vmem_limit_bytes=40 * 1024 * 1024),
        )(places_of(part), depth, first, tables[part])

    if wa_count == 2 and width % LANES == 0:
        parts = width // LANES
        scratch = [
            pltpu.VMEM(shape, jnp.bfloat16),
            pltpu.VMEM((parts, SUB * PITCH, LANES), jnp.float32),
            pltpu.VMEM((parts, 64, SUB, 2 * LANES), jnp.bfloat16),
            pltpu.VMEM((parts, 64, share, LANES), jnp.bfloat16),
            pltpu.VMEM((parts, 64, share, LANES), jnp.bfloat16),
            pltpu.VMEM((parts, share * OUT_PITCH, LANES), jnp.float32),
        ]
        scratch += [pltpu.SemaphoreType.DMA((parts * SWAPS,))] * 2
        scratch += [pltpu.SemaphoreType.DMA((parts * SENDS,))] * 2
        return pl.pallas_call(
            functools.partial(finish_kernel, width),
            out_shape=jax.ShapeDtypeStruct((width, span), jnp.float32),
            in_specs=[smem, smem] + [vmem] * 4,
            out_specs=vmem,
            scratch_shapes=scratch,
            compiler_params=pltpu.CompilerParams(
                collective_id=1, has_side_effects=True, vmem_limit_bytes=24 * 1024 * 1024
            ),
        )(
            places_of(wa_index),
            depth,
            own,
            give,
            jnp.asarray(head_matrices()),
            tables,
        )
    came_half = lax.ppermute(give, "uv", [(n, n ^ 1) for n in range(uv_count)])

    first, part = head_of(jnp.int32(0), jnp.bfloat16)
    images = [part] + [tail_of(jnp.int32(n), first, jnp.bfloat16) for n in range(1, wa_count)]
    parts = jnp.stack(images, axis=1)
    came = lax.all_to_all(parts, "wa", split_axis=1, concat_axis=1)
    return jnp.sum(came.astype(jnp.float32), axis=1)


def solution(mesh):
    in_specs = (
        P(("wa", "uv"), None, None),
        P(("wa", "uv"), None, None),
        P(("wa", "uv"), None),
        P(("wa", "uv")),
        P("wa", "uv"),
    )
    return jax.shard_map(
        on_device, mesh=mesh, in_specs=in_specs, out_specs=P("uv", "wa"), check_vma=False
    )
```

```python
import functools
import math

import jax
import jax.numpy as jnp
import ml_dtypes
import numpy as np
from jax import lax
from jax.experimental import pallas as pl
from jax.experimental.pallas import tpu as pltpu
from jax.sharding import PartitionSpec as P

G = 4096
SUB = 64
BATCH = 8
PLACES = 8
WIPE = 72
STACK = 4
LANES = 128
PITCH = 129
OUT_PITCH = 65
SWAPS = 2
SENDS = 4
plane_step = 6.0
full_turn = 2.0 * math.pi
BF = ml_dtypes.bfloat16


def turn_poly(bound, degree):
    nodes = np.cos(np.pi * (np.arange(256) + 0.5) / 256)
    z = (nodes + 1.0) / (2.0 * bound)
    f = np.sqrt(z)
    cos_c = np.polynomial.chebyshev.cheb2poly(
        np.polynomial.chebyshev.chebfit(nodes, np.cos(2 * np.pi * f), degree)
    )
    sin_c = np.polynomial.chebyshev.cheb2poly(
        np.polynomial.chebyshev.chebfit(nodes, np.sin(2 * np.pi * f) / f, degree)
    )
    base = np.polynomial.Polynomial([-1.0, 2.0 * bound])
    out = []
    for coefs in (cos_c, sin_c):
        total = np.polynomial.Polynomial([0.0])
        for c in coefs[::-1]:
            total = total * base + c
        out.append([float(c) for c in total.coef])
    return out


COS_C, SIN_C = turn_poly(4.0, 5)
COS_S, SIN_S = turn_poly(16.0, 4)


def cos_sin_part(f, cos_c, sin_c):
    z = f * f
    c = cos_c[-1] * z + cos_c[-2]
    for k in cos_c[-3::-1]:
        c = c * z + k
    s = sin_c[-1] * z + sin_c[-2]
    for k in sin_c[-3::-1]:
        s = s * z + k
    return c, s * f


def cos_sin_turns(turns):
    return cos_sin_part(turns - jnp.round(turns), COS_C, SIN_C)


def times(a, b):
    return a[0] * b[0] - a[1] * b[1], a[0] * b[1] + a[1] * b[0]


def squared(a):
    twice = a[0] + a[0]
    return twice * a[0] - 1.0, twice * a[1]


def half_orders():
    fine = np.arange(8) + 0.5
    return np.concatenate([fine, 16 - fine, 16 + fine, 32 - fine])


def dirichlet(x):
    bottom = np.sin(np.pi * x / SUB)
    zero = np.abs(bottom) < 1e-12
    return np.where(zero, float(SUB), np.sin(np.pi * x) / np.where(zero, 1.0, bottom))


def spread_table():
    at = (np.arange(G) - G // 2) / SUB + 0.5
    order = half_orders()[:, None]
    minus, plus = dirichlet(at[None] - order), dirichlet(at[None] + order)
    return np.concatenate([minus + plus, minus - plus], axis=0)


def column_table(devices):
    whole = (spread_table() / SUB).reshape(SUB, devices, G // devices)
    return np.ascontiguousarray(whole.transpose(1, 0, 2)).astype(np.float32)


def row_table(parts):
    whole = (spread_table() / G).reshape(SUB, parts, SUB // parts, 64)
    return np.ascontiguousarray(whole.transpose(1, 3, 2, 0)).astype(BF)


def head_matrices():
    l0 = np.arange(64)[:, None]
    out = []
    for core in range(2):
        columns = []
        for source in range(2):
            t = (2 * np.arange(32) + (core ^ source))[None, :]
            ang = full_turn / 64 * np.mod(l0 * t, 64)
            c, s = np.cos(ang), np.sin(ang)
            columns.append(np.block([[c, -s], [s, c]]))
        out.append(np.concatenate(columns, axis=1))
    return np.stack(out).astype(BF)


def gather_kernel(
    far, near, x_ref, out_ref,
    own_sem, ring_send, ring_recv, side_send, side_recv, core_send, core_recv,
):
    uv = lax.axis_index("uv")
    c = lax.rem(uv, 2)
    b = lax.rem(uv // 2, near)
    a = uv // (2 * near)
    mesh_type = pl.DeviceIdType.MESH
    sources = (x_ref,)
    outs = (out_ref,)

    def at(da, db, dc):
        return ((a + da) * near + lax.rem(b + db + near, near)) * 2 + lax.rem(c + dc, 2)

    def inside(da):
        return jnp.logical_and(a + da >= 0, a + da < far)

    barrier = pltpu.get_barrier_semaphore()

    def greet(device):
        pl.semaphore_signal(barrier, inc=1, device_id={"uv": device}, device_id_type=mesh_type)

    for side in (-1, 1):
        pl.when(inside(side))(lambda side=side: greet(at(side, 0, 0)))
    for e in range(1, near):
        greet(at(0, e, 0))
    greet(at(0, 0, 1))
    mine = [
        pltpu.make_async_copy(sources[k], outs[k].at[uv], own_sem.at[k]) for k in range(1)
    ]
    for one in mine:
        one.start()
    beside = jnp.where(a > 0, 1, 0) + jnp.where(a < far - 1, 1, 0)
    pl.semaphore_wait(barrier, beside + near)

    def copy(k, own, slot, target, send, recv):
        return pltpu.make_async_remote_copy(
            src_ref=sources[k] if own else outs[k].at[slot],
            dst_ref=outs[k].at[slot],
            send_sem=send,
            recv_sem=recv,
            device_id={"uv": target},
            device_id_type=mesh_type,
        )

    first = (0,)
    second = ()
    sends = []

    def start(valid, one):
        pl.when(valid)(lambda: one.start())
        sends.append((valid, one))

    def along(k, da, e, own):
        slot = at(da, -e, 0)
        if da <= 0:
            n = (k * near + e) * 2 * far - da
            start(
                jnp.logical_and(inside(da), inside(1)),
                copy(k, own, slot, at(1, 0, 0), ring_send.at[n], ring_recv.at[n + 1]),
            )
        if da >= 0:
            n = ((k * near + e) * 2 + 1) * far + da
            start(
                jnp.logical_and(inside(da), inside(-1)),
                copy(k, own, slot, at(-1, 0, 0), ring_send.at[n], ring_recv.at[n + 1]),
            )

    def arrived_along(k, da, e):
        slot = at(da, -e, 0)
        n = (k * near + e) * 2 * far - da if da < 0 else ((k * near + e) * 2 + 1) * far + da
        one = copy(k, False, slot, uv ^ 1, ring_send.at[n], ring_recv.at[n])
        pl.when(inside(da))(lambda: one.wait_recv())

    def aside(k, da, own):
        for e in range(1, near):
            n = (k * (2 * far) + far + da) * near + e
            start(
                inside(da),
                copy(k, own, at(da, 0, 0), at(0, e, 0), side_send.at[n], side_recv.at[n]),
            )

    def arrived_aside(k, da, e):
        n = (k * (2 * far) + far + da) * near + e
        one = copy(k, False, at(da, -e, 0), uv ^ 1, side_send.at[n], side_recv.at[n])
        pl.when(inside(da))(lambda: one.wait_recv())

    def across(k, da, e, own):
        n = (k * (2 * far) + far + da) * near + e
        start(
            inside(da),
            copy(k, own, at(da, -e, 0), at(0, 0, 1), core_send.at[n], core_recv.at[n]),
        )

    for k in second:
        aside(k, 0, True)
    for k in first:
        along(k, 0, 0, True)
    for k in second:
        along(k, 0, 0, True)
    for k in first:
        aside(k, 0, True)
    for k in range(1):
        across(k, 0, 0, True)
    for e in range(1, near):
        for k in second:
            arrived_aside(k, 0, e)
            along(k, 0, e, False)
            across(k, 0, e, False)
    for s in range(1, far):
        for k in first:
            for da in (-s, s):
                arrived_along(k, da, 0)
                along(k, da, 0, False)
                aside(k, da, False)
                across(k, da, 0, False)
        for e in range(near):
            for k in second:
                for da in (-s, s):
                    arrived_along(k, da, e)
                    along(k, da, e, False)
                    across(k, da, e, False)
    for k in first:
        for da in sorted(range(1 - far, far), key=abs):
            for e in range(1, near):
                arrived_aside(k, da, e)
                across(k, da, e, False)
    for da in sorted(range(1 - far, far), key=abs):
        for e in range(near):
            for k in range(1):
                n = (k * (2 * far) + far + da) * near + e
                one = copy(k, False, at(da, -e, 1), uv ^ 1, core_send.at[n], core_recv.at[n])
                pl.when(inside(da))(lambda one=one: one.wait_recv())
    for one in mine:
        one.wait()
    for valid, one in sends:
        pl.when(valid)(lambda one=one: one.wait_send())


def gather_all(packed, uv_count):
    chips = uv_count // 2
    near = 1 << ((chips.bit_length() - 1) // 2)
    far = chips // near
    sems = [1] + [near * 2 * far + 1] * 2 + [2 * far * near] * 4
    return pl.pallas_call(
        functools.partial(gather_kernel, far, near),
        out_shape=jax.ShapeDtypeStruct((uv_count,) + packed.shape, packed.dtype),
        in_specs=[pl.BlockSpec(memory_space=pltpu.VMEM)],
        out_specs=pl.BlockSpec(memory_space=pltpu.VMEM),
        scratch_shapes=[pltpu.SemaphoreType.DMA((n,)) for n in sems],
        compiler_params=pltpu.CompilerParams(
            collective_id=0, has_side_effects=True, vmem_limit_bytes=16 * 1024 * 1024
        ),
    )(packed)


def grid_kernel(
    width, blocks, homes, cols, counts, data_ref, m_ref, d_all, keep_ref, give_ref,
    acc, slots, filled, fours, twos, d_ref, *buffers,
):
    each = 2 * blocks + 2
    devices = data_ref.shape[0] // each
    k_len = data_ref.shape[2]
    cap = 2 * devices
    half_tiles = G // SUB // 2
    both = 2 * width
    k_parts = k_len // LANES
    m_parts = both // LANES
    uv = lax.axis_index("uv")
    stage = buffers[0]
    sets = (buffers[1:5], buffers[5:9])
    d_ref[:, :width] = d_all[uv]
    d_ref[:, width:] = d_all[uv + 1 - 2 * lax.rem(uv, 2)]

    for n in range(3):
        fours[n] = 0
        twos[n] = 0

    def empty(h, carry):
        filled[h] = 0
        return carry

    lax.fori_loop(0, half_tiles + 1, empty, 0)
    wipes = acc.shape[1] // WIPE

    def wipe(n):
        at = pl.multiple_of(jnp.minimum(n, wipes - 1) * WIPE, WIPE)
        for c in range(2 * m_parts):
            acc[c, pl.ds(at, WIPE), :] = jnp.zeros((WIPE, LANES), jnp.float32)


    def spread(j, carry):
        def place(n, inner):
            wipe(inner)
            for k in range(PLACES):
                i = n * PLACES + k
                h = homes[j * blocks + i]
                n_h = filled[h]
                slots[h * cap + n_h] = j * each + i
                filled[h] = n_h + 1
            return inner + 1

        return lax.fori_loop(0, (counts[j] + PLACES - 1) // PLACES, place, carry)

    def wipe_rest(n, carry):
        wipe(n)
        return carry

    lax.fori_loop(lax.fori_loop(0, devices, spread, 0), wipes, wipe_rest, 0)

    def list_groups(h, found):
        count = filled[h]
        whole = (count + 1) // STACK

        def one(g, n):
            fours[3 * n] = h
            fours[3 * n + 1] = h * cap + STACK * g
            fours[3 * n + 2] = count - STACK * g
            return n + 1

        n, m = found
        n = lax.fori_loop(0, whole, one, n)
        rest = count - STACK * whole
        twos[3 * m] = h
        twos[3 * m + 1] = h * cap + STACK * whole
        twos[3 * m + 2] = rest
        return n, m + jnp.where(rest > 0, 1, 0)

    n_fours, n_twos = lax.fori_loop(0, half_tiles, list_groups, (0, 0))
    scale = 1.0 / math.sqrt(k_len)

    def prepare(batch, refs, stack, group, total):
        fine, coarse, signal, phase = refs
        for p in range(BATCH // stack):
            n = batch * (BATCH // stack) + p
            real = n < total
            n = jnp.where(real, n, 0)
            first = group[3 * n + 1]
            left_over = jnp.where(real, group[3 * n + 2], 0)
            for q in range(stack):
                live = q < left_over
                row = jnp.where(live, slots[first + q], 0)
                centre = (2 * cols[row] - (G - SUB + 1)).astype(jnp.float32)
                keep = jnp.where(live, scale, 0.0)
                k = p * stack + q
                signals = data_ref[row].astype(jnp.float32) * keep
                places = data_ref[row + blocks].astype(jnp.float32)
                for c in range(k_parts):
                    cut = slice(c * LANES, (c + 1) * LANES)
                    for r in range(2):
                        stage[r, c, k : k + 1, :] = signals[r : r + 1, cut]
                        stage[2 + r, c, k : k + 1, :] = places[r : r + 1, cut]
                stage[4, 0, k : k + 1, :] = jnp.full((1, LANES), centre, jnp.float32)
        for c in range(k_parts):
            halves = []
            for axis in range(2):
                turns = (stage[2 + axis, c] + 0.5) * (0.5 / SUB)
                half = cos_sin_part(turns, COS_S, SIN_S)
                halves.append(half)
                step = squared(half)
                power = half
                for b in range(8):
                    if b:
                        power = times(power, step)
                    for e in range(2):
                        fine[axis, e, c, b * 9 : b * 9 + 8, :] = power[e]
                power = squared(times(power, half))
                for e in range(2):
                    coarse[4 * axis + e, c] = power[e]
                power = squared(power)
                for e in range(2):
                    coarse[4 * axis + 2 + e, c] = power[e]
            hc, hs = times(*halves)
            vr, vi = stage[0, c], stage[1, c]
            signal[0, c] = vr * hc + vi * hs
            wi = vi * hc - vr * hs
            signal[1, c] = wi
            signal[2, c] = -wi
        for c in range(m_parts):
            pc, ps = cos_sin_turns(stage[4, 0] * m_ref[:, c * LANES : (c + 1) * LANES])
            phase[0, c] = pc
            phase[1, c] = ps
            phase[2, c] = -ps

    def expand(c, s, c1, s1, c2, s2):
        a, b, d, e = c1 * c, s1 * s, s1 * c, c1 * s
        return (
            jnp.concatenate([c, a + b, a - b, c2 * c + s2 * s], axis=0),
            jnp.concatenate([s, d - e, d + e, s2 * c - c2 * s], axis=0),
        )

    def piece_of(k, refs):
        fine, coarse, signal, _ = refs
        lefts, rights = [], []
        for c in range(k_parts):
            tables = []
            for axis in range(2):
                start = [fine[axis, e, c, pl.ds(k, 8, stride=9), :] for e in range(2)]
                rows = [coarse[4 * axis + n, c, k : k + 1, :] for n in range(4)]
                tables.append(expand(*start, *rows))
            (cu, su), (cv, sv) = tables
            wr, wi, nwi = (signal[n, c, k : k + 1, :] for n in range(3))
            lefts.append(
                jnp.concatenate([wr * cu, nwi * su, wi * cu, wr * su], axis=0).astype(jnp.bfloat16)
            )
            rights.append(jnp.concatenate([cv, sv], axis=0).astype(jnp.bfloat16))
        return lax.dot_general(
            jnp.concatenate(lefts, axis=1),
            jnp.concatenate(rights, axis=1),
            (((1,), (1,)), ((), ())),
            preferred_element_type=jnp.float32,
        ).astype(jnp.bfloat16)

    def gather_up(batch, refs, stack, group, total):
        phase = refs[3]
        pieces = [
            jnp.concatenate([piece_of(k, refs) for k in range(p * stack, (p + 1) * stack)], axis=1)
            for p in range(BATCH // stack)
        ]
        for p in range(BATCH // stack):
            n = batch * (BATCH // stack) + p
            h = group[3 * jnp.where(n < total, n, 0)]
            rows = pl.ds(h * PITCH, 2 * SUB)
            ks = range(p * stack, (p + 1) * stack)
            piece = pieces[p]
            wide = min(2, m_parts)
            for c0 in range(0, m_parts, wide):
                tops = [d_ref[:32, c * LANES : (c + 1) * LANES] for c in range(c0, c0 + wide)]
                lows = [d_ref[32:, c * LANES : (c + 1) * LANES] for c in range(c0, c0 + wide)]
                for turn in range(2):
                    weight = []
                    for k in ks:
                        top, low = [], []
                        for c in range(c0, c0 + wide):
                            pr, pi, npi = (phase[e, c, k : k + 1, :] for e in range(3))
                            top.append(tops[c - c0] * (pi if turn else pr))
                            low.append(lows[c - c0] * (pr if turn else npi))
                        weight += [jnp.concatenate(top, axis=1), jnp.concatenate(low, axis=1)]
                    got = jnp.dot(
                        piece,
                        jnp.concatenate(weight, axis=0).astype(jnp.bfloat16),
                        preferred_element_type=jnp.float32,
                    )
                    for c in range(wide):
                        at = turn * m_parts + c0 + c
                        acc[at, rows, :] += got[:, c * LANES : (c + 1) * LANES]

    for stack, group, total in ((STACK, fours, n_fours), (2, twos, n_twos)):
        batches = (total + BATCH // stack - 1) // (BATCH // stack)
        rest = (stack, group, total)
        prepare(0, sets[0], *rest)

        def step(it, carry, rest=rest):
            for n in range(2):
                gather_up(2 * it + n, sets[n], *rest)
                prepare(2 * it + n + 1, sets[1 - n], *rest)
            return carry

        lax.fori_loop(0, batches // 2, step, 0)

        def last(it, carry, rest=rest, batches=batches):
            gather_up(batches - 1, sets[0], *rest)
            return carry

        lax.fori_loop(0, lax.rem(batches, 2), last, 0)

    def turned(lam, carry):
        top = [acc[c, pl.ds(lam, half_tiles, stride=PITCH), :] for c in range(2 * m_parts)]
        low = [acc[c, pl.ds(SUB + lam, half_tiles, stride=PITCH), :] for c in range(2 * m_parts)]
        re = [top[c] - low[m_parts + c] for c in range(m_parts)]
        im = [top[m_parts + c] + low[c] for c in range(m_parts)]
        if width < LANES:
            re = [re[0][:, :width], re[0][:, width:]]
            im = [im[0][:, :width], im[0][:, width:]]
        whole = [jnp.concatenate(x, axis=0).astype(jnp.bfloat16) for x in zip(re, im)]
        parts = len(whole) // 2
        for c in range(parts):
            keep_ref[c, lam] = whole[c]
            give_ref[c, lam] = whole[parts + c]
        return carry

    lax.fori_loop(0, SUB, turned, 0, unroll=4)


def in_lanes(rows):
    width = rows.shape[1]
    if width < LANES:
        return [jnp.concatenate([rows] * (LANES // width), axis=1)]
    return [rows[:, c : c + LANES] for c in range(0, width, LANES)]


def lane_chunks(width):
    return max(1, width // LANES)


def tail_rows(width, share, place, y_of, table, out_t):
    part, depth, m_first = place

    def step(l0, carry):
        z = jnp.dot(table[l0], y_of(l0), preferred_element_type=jnp.float32)
        l1 = part * share + lax.broadcasted_iota(jnp.int32, (share, width), 0)
        l = l0 + 64 * l1 - G // 2
        m = m_first + lax.broadcasted_iota(jnp.int32, (share, width), 1)
        x = l.astype(jnp.float32) * (1.0 / G)
        y = m.astype(jnp.float32) * (1.0 / G)
        ramp = jnp.bitwise_and(-(G - SUB + 1) * l, 2 * G - 1).astype(jnp.float32) * (0.5 / G)
        sc, ss = cos_sin_turns(depth * (jnp.sqrt(1.0 - y * y - x * x) - 1.0) + ramp)
        for c, rows in enumerate(in_lanes(z[:, :width] * sc - z[:, width:] * ss)):
            out_t[c, pl.ds(l0, share, stride=64), :] = rows
        return carry

    lax.fori_loop(0, 64, step, 0, unroll=4)


def turn_out(out_t, out_ref):
    chunk = 128

    def step(n, carry):
        at = pl.multiple_of(n * chunk, chunk)
        for c in range(out_t.shape[0]):
            turned = out_t[c, pl.ds(at, chunk), :].T.astype(out_ref.dtype)
            width = min(LANES, out_ref.shape[0])
            out_ref[c * width : (c + 1) * width, pl.ds(at, chunk)] = turned[:width]
        return carry

    lax.fori_loop(0, out_t.shape[1] // chunk, step, 0, unroll=4)


def head_kernel(
    width, share, places, depths, own_ref, came_ref, head_ref, table, y_ref, out_ref, mid, out_t
):
    def head(lam, carry):
        rhs = jnp.concatenate([own_ref[0, lam], came_ref[0, lam]], axis=0)
        got = jnp.dot(head_ref[...], rhs, preferred_element_type=jnp.float32)
        for c, rows in enumerate(in_lanes(got)):
            mid[c, pl.ds(lam * PITCH, 128), :] = rows
        return carry

    lax.fori_loop(0, SUB, head, 0, unroll=4)

    def y_of(l0):
        halves = []
        for first in (0, 64):
            rows = [mid[c, pl.ds(first + l0, SUB, stride=PITCH), :] for c in range(mid.shape[0])]
            halves += [r[:, : min(width, LANES)] for r in rows]
        y = jnp.concatenate(halves, axis=1).astype(jnp.bfloat16)
        y_ref[l0] = y
        return y

    tail_rows(width, share, (places[0], depths[0], places[1]), y_of, table, out_t)
    turn_out(out_t, out_ref)


def tail_kernel(width, share, places, depths, y_ref, table, out_ref, out_t):
    tail_rows(
        width, share, (places[0], depths[0], places[1]), lambda l0: y_ref[l0], table, out_t
    )
    turn_out(out_t, out_ref)


def finish_kernel(
    width, places, depths, keep_ref, give_ref, head_all, table,
    out_ref, came, mid, y_buf, away, other, out_t, core_send, core_recv, far_send, far_recv,
):
    uv = lax.axis_index("uv")
    wa = lax.axis_index("wa")
    near = {"uv": uv + 1 - 2 * lax.rem(uv, 2)}
    far = {"wa": 1 - wa}
    mesh_type = pl.DeviceIdType.MESH
    barrier = pltpu.get_barrier_semaphore()
    pl.semaphore_signal(barrier, inc=1, device_id=near, device_id_type=mesh_type)
    pl.semaphore_signal(barrier, inc=1, device_id=far, device_id_type=mesh_type)
    pl.semaphore_wait(barrier, 2)

    parts = width // LANES
    lam_step = SUB // SWAPS
    swaps = []
    for c in range(parts):
        for k in range(SWAPS):
            at = pl.ds(k * lam_step, lam_step)
            n = c * SWAPS + k
            swaps.append(
                pltpu.make_async_remote_copy(
                    src_ref=give_ref.at[c, at],
                    dst_ref=came.at[c, at],
                    send_sem=core_send.at[n],
                    recv_sem=core_recv.at[n],
                    device_id=near,
                    device_id_type=mesh_type,
                )
            )
            swaps[-1].start()
    core = lax.rem(uv, 2)

    share = SUB // 2
    step = 64 // SENDS

    def screened(c, l0, part, z):
        l1 = part * share + lax.broadcasted_iota(jnp.int32, (share, LANES), 0)
        l = l0 + 64 * l1 - G // 2
        m = places[1] + c * LANES + lax.broadcasted_iota(jnp.int32, (share, LANES), 1)
        x = l.astype(jnp.float32) * (1.0 / G)
        y = m.astype(jnp.float32) * (1.0 / G)
        ramp = jnp.bitwise_and(-(G - SUB + 1) * l, 2 * G - 1).astype(jnp.float32) * (0.5 / G)
        sc, ss = cos_sin_turns(depths[0] * (jnp.sqrt(1.0 - y * y - x * x) - 1.0) + ramp)
        return z[:, :LANES] * sc - z[:, LANES:] * ss

    sends = []
    for c in range(parts):

        def head(lam, carry, c=c):
            rhs = jnp.concatenate([keep_ref[c, lam], came[c, lam]], axis=0)
            mid[c, pl.ds(lam * PITCH, 128), :] = jnp.dot(
                head_all[core], rhs, preferred_element_type=jnp.float32
            )
            return carry

        for k in range(SWAPS):
            swaps[c * SWAPS + k].wait_recv()
            lax.fori_loop(k * lam_step, (k + 1) * lam_step, head, 0, unroll=16)

        def away_rows(l0, carry, c=c):
            y = jnp.concatenate(
                [mid[c, pl.ds(first + l0, SUB, stride=PITCH), :] for first in (0, 64)], axis=1
            ).astype(jnp.bfloat16)
            y_buf[c, l0] = y
            z = jnp.dot(table[1 - wa, l0], y, preferred_element_type=jnp.float32)
            away[c, l0] = screened(c, l0, 1 - places[0], z).astype(jnp.bfloat16)
            return carry

        for k in range(SENDS):
            lax.fori_loop(k * step, (k + 1) * step, away_rows, 0, unroll=16)
            at = pl.ds(k * step, step)
            n = c * SENDS + k
            sends.append(
                pltpu.make_async_remote_copy(
                    src_ref=away.at[c, at],
                    dst_ref=other.at[c, at],
                    send_sem=far_send.at[n],
                    recv_sem=far_recv.at[n],
                    device_id=far,
                    device_id_type=mesh_type,
                )
            )
            sends[-1].start()

    for c in range(parts):

        def own_rows(l0, carry, c=c):
            z = jnp.dot(table[wa, l0], y_buf[c, l0], preferred_element_type=jnp.float32)
            out_t[c, pl.ds(l0, share, stride=OUT_PITCH), :] = screened(c, l0, places[0], z)
            return carry

        lax.fori_loop(0, 64, own_rows, 0, unroll=16)

    for c in range(parts):

        def add_rows(l0, carry, c=c):
            at = pl.ds(l0, share, stride=OUT_PITCH)
            out_t[c, at, :] += other[c, l0].astype(jnp.float32)
            return carry

        for k in range(SENDS):
            sends[c * SENDS + k].wait_recv()
            lax.fori_loop(k * step, (k + 1) * step, add_rows, 0, unroll=16)

        for n in range(share // 2):
            rows = [out_t[c, pl.ds((2 * n + h) * OUT_PITCH, 64), :] for h in range(2)]
            out_ref[c * LANES : (c + 1) * LANES, n * LANES : (n + 1) * LANES] = jnp.concatenate(
                rows, axis=0
            ).T
    for one in swaps + sends:
        one.wait_send()


def on_device(visibility, coords, tile_row, col_offset, live_count):
    uv_count = lax.axis_size("uv")
    wa_count = lax.axis_size("wa")
    uv_index = lax.axis_index("uv")
    wa_index = lax.axis_index("wa")
    blocks = visibility.shape[0]
    k_len = visibility.shape[2]
    width = G // uv_count
    core = jnp.mod(uv_index, 2)
    partner = uv_index + 1 - 2 * core
    m_first = uv_index * width - G // 2
    m_both = jnp.concatenate(
        [m_first + jnp.arange(width), partner * width + jnp.arange(width) - G // 2]
    )[None, :].astype(jnp.float32) * (0.5 / G)
    given = lax.optimization_barrier(
        jnp.concatenate([tile_row.reshape(1, blocks), col_offset.reshape(1, blocks)], axis=0)
    )
    numbers = jnp.stack(
        [
            given[0],
            given[1] // SUB,
            jnp.bitwise_and(given[1], SUB - 1),
            jnp.broadcast_to(live_count[0], (blocks,)),
        ]
    )
    numbers = jnp.pad(numbers, ((0, 0), (0, k_len - blocks))).astype(jnp.bfloat16)
    packed = jnp.concatenate([visibility, coords, numbers.reshape(2, 2, k_len)], axis=0)
    all_data = gather_all(packed, uv_count)
    numbers = all_data[:, 2 * blocks :, :, :blocks].reshape(uv_count, 4, blocks)
    numbers = numbers.astype(jnp.int32)
    tiles = numbers[:, 0]
    cols = numbers[:, 1] * SUB + numbers[:, 2]
    cols = jnp.pad(cols, ((0, 0), (0, blocks + 2))).reshape(-1)
    live = jnp.arange(blocks)[None, :] < numbers[:, 3]
    mine = live & (jnp.mod(tiles, 2) == core)
    homes = jnp.where(mine, tiles // 2, G // SUB // 2).reshape(-1)
    half_tiles = G // SUB // 2
    cap = 2 * uv_count
    shape = (lane_chunks(width), SUB, SUB, min(width, LANES))
    vmem = pl.BlockSpec(memory_space=pltpu.VMEM)
    smem = pl.BlockSpec(memory_space=pltpu.SMEM)
    m_parts = 2 * width // LANES
    k_parts = k_len // LANES
    buffers = [
        pltpu.VMEM((2, 2, k_parts, 72, LANES), jnp.float32),
        pltpu.VMEM((8, k_parts, BATCH, LANES), jnp.float32),
        pltpu.VMEM((3, k_parts, BATCH, LANES), jnp.float32),
        pltpu.VMEM((3, m_parts, BATCH, LANES), jnp.float32),
    ]
    own, give = pl.pallas_call(
        functools.partial(grid_kernel, width, blocks),
        out_shape=[jax.ShapeDtypeStruct(shape, jnp.bfloat16)] * 2,
        in_specs=[smem, smem, smem, vmem, vmem, vmem],
        out_specs=[vmem, vmem],
        scratch_shapes=[
            pltpu.VMEM((2 * m_parts, -(-half_tiles * PITCH // WIPE) * WIPE, LANES), jnp.float32),
            pltpu.SMEM((half_tiles * cap + uv_count * blocks,), jnp.int32),
            pltpu.SMEM((half_tiles + 1,), jnp.int32),
            pltpu.SMEM((3 * (uv_count * blocks // STACK + half_tiles),), jnp.int32),
            pltpu.SMEM((3 * (half_tiles + 1),), jnp.int32),
            pltpu.VMEM((SUB, 2 * width), jnp.float32),
            pltpu.VMEM((5, k_parts, BATCH, LANES), jnp.float32),
        ]
        + buffers
        + buffers,
        compiler_params=pltpu.CompilerParams(vmem_limit_bytes=32 * 1024 * 1024),
    )(
        homes,
        cols,
        numbers[:, 3, 0],
        all_data.reshape((-1,) + all_data.shape[2:]),
        m_both,
        jnp.asarray(column_table(uv_count)),
    )
    share = 64 // wa_count
    depth = ((wa_index.astype(jnp.float32) - (wa_count - 1) / 2.0) * plane_step)[None]
    tables = jnp.asarray(row_table(wa_count))
    span = G // wa_count

    def places_of(part):
        return jnp.stack([part, m_first]).astype(jnp.int32)

    def head_of(part, dtype):
        return pl.pallas_call(
            functools.partial(head_kernel, width, share),
            out_shape=[
                jax.ShapeDtypeStruct((64, SUB, 2 * width), jnp.bfloat16),
                jax.ShapeDtypeStruct((width, span), dtype),
            ],
            in_specs=[smem, smem, vmem, vmem, vmem, vmem],
            out_specs=[vmem, vmem],
            scratch_shapes=[
                pltpu.VMEM((lane_chunks(width), SUB * PITCH, LANES), jnp.float32),
                pltpu.VMEM((lane_chunks(width), span, LANES), jnp.float32),
            ],
            compiler_params=pltpu.CompilerParams(vmem_limit_bytes=40 * 1024 * 1024),
        )(
            places_of(part), depth, own, came_half, jnp.asarray(head_matrices())[core], tables[part]
        )

    def tail_of(part, first, dtype):
        return pl.pallas_call(
            functools.partial(tail_kernel, width, share),
            out_shape=jax.ShapeDtypeStruct((width, span), dtype),
            in_specs=[smem, smem, vmem, vmem],
            out_specs=vmem,
            scratch_shapes=[pltpu.VMEM((lane_chunks(width), span, LANES), jnp.float32)],
            compiler_params=pltpu.CompilerParams(vmem_limit_bytes=40 * 1024 * 1024),
        )(places_of(part), depth, first, tables[part])

    if wa_count == 2 and width % LANES == 0:
        parts = width // LANES
        scratch = [
            pltpu.VMEM(shape, jnp.bfloat16),
            pltpu.VMEM((parts, SUB * PITCH, LANES), jnp.float32),
            pltpu.VMEM((parts, 64, SUB, 2 * LANES), jnp.bfloat16),
            pltpu.VMEM((parts, 64, share, LANES), jnp.bfloat16),
            pltpu.VMEM((parts, 64, share, LANES), jnp.bfloat16),
            pltpu.VMEM((parts, share * OUT_PITCH, LANES), jnp.float32),
        ]
        scratch += [pltpu.SemaphoreType.DMA((parts * SWAPS,))] * 2
        scratch += [pltpu.SemaphoreType.DMA((parts * SENDS,))] * 2
        return pl.pallas_call(
            functools.partial(finish_kernel, width),
            out_shape=jax.ShapeDtypeStruct((width, span), jnp.float32),
            in_specs=[smem, smem] + [vmem] * 4,
            out_specs=vmem,
            scratch_shapes=scratch,
            compiler_params=pltpu.CompilerParams(
                collective_id=1, has_side_effects=True, vmem_limit_bytes=24 * 1024 * 1024
            ),
        )(
            places_of(wa_index),
            depth,
            own,
            give,
            jnp.asarray(head_matrices()),
            tables,
        )
    came_half = lax.ppermute(give, "uv", [(n, n ^ 1) for n in range(uv_count)])

    first, part = head_of(jnp.int32(0), jnp.bfloat16)
    images = [part] + [tail_of(jnp.int32(n), first, jnp.bfloat16) for n in range(1, wa_count)]
    parts = jnp.stack(images, axis=1)
    came = lax.all_to_all(parts, "wa", split_axis=1, concat_axis=1)
    return jnp.sum(came.astype(jnp.float32), axis=1)


def solution(mesh):
    in_specs = (
        P(("wa", "uv"), None, None),
        P(("wa", "uv"), None, None),
        P(("wa", "uv"), None),
        P(("wa", "uv")),
        P("wa", "uv"),
    )
    return jax.shard_map(
        on_device, mesh=mesh, in_specs=in_specs, out_specs=P("uv", "wa"), check_vma=False
    )
```

```python
import functools
import math

import jax
import jax.numpy as jnp
import ml_dtypes
import numpy as np
from jax import lax
from jax.experimental import pallas as pl
from jax.experimental.pallas import tpu as pltpu
from jax.sharding import PartitionSpec as P

G = 4096
SUB = 64
BATCH = 8
PLACES = 8
WIPE = 72
STACK = 4
LANES = 128
PITCH = 129
OUT_PITCH = 65
SWAPS = 4
SENDS = 8
plane_step = 6.0
full_turn = 2.0 * math.pi
BF = ml_dtypes.bfloat16


def turn_poly(bound, degree):
    nodes = np.cos(np.pi * (np.arange(256) + 0.5) / 256)
    z = (nodes + 1.0) / (2.0 * bound)
    f = np.sqrt(z)
    cos_c = np.polynomial.chebyshev.cheb2poly(
        np.polynomial.chebyshev.chebfit(nodes, np.cos(2 * np.pi * f), degree)
    )
    sin_c = np.polynomial.chebyshev.cheb2poly(
        np.polynomial.chebyshev.chebfit(nodes, np.sin(2 * np.pi * f) / f, degree)
    )
    base = np.polynomial.Polynomial([-1.0, 2.0 * bound])
    out = []
    for coefs in (cos_c, sin_c):
        total = np.polynomial.Polynomial([0.0])
        for c in coefs[::-1]:
            total = total * base + c
        out.append([float(c) for c in total.coef])
    return out


COS_C, SIN_C = turn_poly(4.0, 5)
COS_S, SIN_S = turn_poly(16.0, 4)


def cos_sin_part(f, cos_c, sin_c):
    z = f * f
    c = cos_c[-1] * z + cos_c[-2]
    for k in cos_c[-3::-1]:
        c = c * z + k
    s = sin_c[-1] * z + sin_c[-2]
    for k in sin_c[-3::-1]:
        s = s * z + k
    return c, s * f


def cos_sin_turns(turns):
    return cos_sin_part(turns - jnp.round(turns), COS_C, SIN_C)


def times(a, b):
    return a[0] * b[0] - a[1] * b[1], a[0] * b[1] + a[1] * b[0]


def squared(a):
    twice = a[0] + a[0]
    return twice * a[0] - 1.0, twice * a[1]


def half_orders():
    fine = np.arange(8) + 0.5
    return np.concatenate([fine, 16 - fine, 16 + fine, 32 - fine])


def dirichlet(x):
    bottom = np.sin(np.pi * x / SUB)
    zero = np.abs(bottom) < 1e-12
    return np.where(zero, float(SUB), np.sin(np.pi * x) / np.where(zero, 1.0, bottom))


def spread_table():
    at = (np.arange(G) - G // 2) / SUB + 0.5
    order = half_orders()[:, None]
    minus, plus = dirichlet(at[None] - order), dirichlet(at[None] + order)
    return np.concatenate([minus + plus, minus - plus], axis=0)


def column_table(devices):
    whole = (spread_table() / SUB).reshape(SUB, devices, G // devices)
    return np.ascontiguousarray(whole.transpose(1, 0, 2)).astype(np.float32)


def row_table(parts):
    whole = (spread_table() / G).reshape(SUB, parts, SUB // parts, 64)
    return np.ascontiguousarray(whole.transpose(1, 3, 2, 0)).astype(BF)


def head_matrices():
    l0 = np.arange(64)[:, None]
    out = []
    for core in range(2):
        columns = []
        for source in range(2):
            t = (2 * np.arange(32) + (core ^ source))[None, :]
            ang = full_turn / 64 * np.mod(l0 * t, 64)
            c, s = np.cos(ang), np.sin(ang)
            columns.append(np.block([[c, -s], [s, c]]))
        out.append(np.concatenate(columns, axis=1))
    return np.stack(out).astype(BF)


def gather_kernel(
    far, near, x_ref, out_ref,
    own_sem, ring_send, ring_recv, side_send, side_recv, core_send, core_recv,
):
    uv = lax.axis_index("uv")
    c = lax.rem(uv, 2)
    b = lax.rem(uv // 2, near)
    a = uv // (2 * near)
    mesh_type = pl.DeviceIdType.MESH
    sources = (x_ref,)
    outs = (out_ref,)

    def at(da, db, dc):
        return ((a + da) * near + lax.rem(b + db + near, near)) * 2 + lax.rem(c + dc, 2)

    def inside(da):
        return jnp.logical_and(a + da >= 0, a + da < far)

    barrier = pltpu.get_barrier_semaphore()

    def greet(device):
        pl.semaphore_signal(barrier, inc=1, device_id={"uv": device}, device_id_type=mesh_type)

    for side in (-1, 1):
        pl.when(inside(side))(lambda side=side: greet(at(side, 0, 0)))
    for e in range(1, near):
        greet(at(0, e, 0))
    greet(at(0, 0, 1))
    mine = [
        pltpu.make_async_copy(sources[k], outs[k].at[uv], own_sem.at[k]) for k in range(1)
    ]
    for one in mine:
        one.start()
    beside = jnp.where(a > 0, 1, 0) + jnp.where(a < far - 1, 1, 0)
    pl.semaphore_wait(barrier, beside + near)

    def copy(k, own, slot, target, send, recv):
        return pltpu.make_async_remote_copy(
            src_ref=sources[k] if own else outs[k].at[slot],
            dst_ref=outs[k].at[slot],
            send_sem=send,
            recv_sem=recv,
            device_id={"uv": target},
            device_id_type=mesh_type,
        )

    first = (0,)
    second = ()
    sends = []

    def start(valid, one):
        pl.when(valid)(lambda: one.start())
        sends.append((valid, one))

    def along(k, da, e, own):
        slot = at(da, -e, 0)
        if da <= 0:
            n = (k * near + e) * 2 * far - da
            start(
                jnp.logical_and(inside(da), inside(1)),
                copy(k, own, slot, at(1, 0, 0), ring_send.at[n], ring_recv.at[n + 1]),
            )
        if da >= 0:
            n = ((k * near + e) * 2 + 1) * far + da
            start(
                jnp.logical_and(inside(da), inside(-1)),
                copy(k, own, slot, at(-1, 0, 0), ring_send.at[n], ring_recv.at[n + 1]),
            )

    def arrived_along(k, da, e):
        slot = at(da, -e, 0)
        n = (k * near + e) * 2 * far - da if da < 0 else ((k * near + e) * 2 + 1) * far + da
        one = copy(k, False, slot, uv ^ 1, ring_send.at[n], ring_recv.at[n])
        pl.when(inside(da))(lambda: one.wait_recv())

    def aside(k, da, own):
        for e in range(1, near):
            n = (k * (2 * far) + far + da) * near + e
            start(
                inside(da),
                copy(k, own, at(da, 0, 0), at(0, e, 0), side_send.at[n], side_recv.at[n]),
            )

    def arrived_aside(k, da, e):
        n = (k * (2 * far) + far + da) * near + e
        one = copy(k, False, at(da, -e, 0), uv ^ 1, side_send.at[n], side_recv.at[n])
        pl.when(inside(da))(lambda: one.wait_recv())

    def across(k, da, e, own):
        n = (k * (2 * far) + far + da) * near + e
        start(
            inside(da),
            copy(k, own, at(da, -e, 0), at(0, 0, 1), core_send.at[n], core_recv.at[n]),
        )

    for k in second:
        aside(k, 0, True)
    for k in first:
        along(k, 0, 0, True)
    for k in second:
        along(k, 0, 0, True)
    for k in first:
        aside(k, 0, True)
    for k in range(1):
        across(k, 0, 0, True)
    for e in range(1, near):
        for k in second:
            arrived_aside(k, 0, e)
            along(k, 0, e, False)
            across(k, 0, e, False)
    for s in range(1, far):
        for k in first:
            for da in (-s, s):
                arrived_along(k, da, 0)
                along(k, da, 0, False)
                aside(k, da, False)
                across(k, da, 0, False)
        for e in range(near):
            for k in second:
                for da in (-s, s):
                    arrived_along(k, da, e)
                    along(k, da, e, False)
                    across(k, da, e, False)
    for k in first:
        for da in sorted(range(1 - far, far), key=abs):
            for e in range(1, near):
                arrived_aside(k, da, e)
                across(k, da, e, False)
    for da in sorted(range(1 - far, far), key=abs):
        for e in range(near):
            for k in range(1):
                n = (k * (2 * far) + far + da) * near + e
                one = copy(k, False, at(da, -e, 1), uv ^ 1, core_send.at[n], core_recv.at[n])
                pl.when(inside(da))(lambda one=one: one.wait_recv())
    for one in mine:
        one.wait()
    for valid, one in sends:
        pl.when(valid)(lambda one=one: one.wait_send())


def gather_all(packed, uv_count):
    chips = uv_count // 2
    near = 1 << ((chips.bit_length() - 1) // 2)
    far = chips // near
    sems = [1] + [near * 2 * far + 1] * 2 + [2 * far * near] * 4
    return pl.pallas_call(
        functools.partial(gather_kernel, far, near),
        out_shape=jax.ShapeDtypeStruct((uv_count,) + packed.shape, packed.dtype),
        in_specs=[pl.BlockSpec(memory_space=pltpu.VMEM)],
        out_specs=pl.BlockSpec(memory_space=pltpu.VMEM),
        scratch_shapes=[pltpu.SemaphoreType.DMA((n,)) for n in sems],
        compiler_params=pltpu.CompilerParams(
            collective_id=0, has_side_effects=True, vmem_limit_bytes=16 * 1024 * 1024
        ),
    )(packed)


def grid_kernel(
    width, blocks, homes, cols, counts, data_ref, m_ref, d_all, keep_ref, give_ref,
    acc, slots, filled, fours, twos, d_ref, *buffers,
):
    each = 2 * blocks + 2
    devices = data_ref.shape[0] // each
    k_len = data_ref.shape[2]
    cap = 2 * devices
    half_tiles = G // SUB // 2
    both = 2 * width
    k_parts = k_len // LANES
    m_parts = both // LANES
    uv = lax.axis_index("uv")
    stage = buffers[0]
    sets = (buffers[1:5], buffers[5:9])
    d_ref[:, :width] = d_all[uv]
    d_ref[:, width:] = d_all[uv + 1 - 2 * lax.rem(uv, 2)]

    for n in range(3):
        fours[n] = 0
        twos[n] = 0

    def empty(h, carry):
        filled[h] = 0
        return carry

    lax.fori_loop(0, half_tiles + 1, empty, 0)
    wipes = acc.shape[1] // WIPE

    def wipe(n):
        at = pl.multiple_of(jnp.minimum(n, wipes - 1) * WIPE, WIPE)
        for c in range(2 * m_parts):
            acc[c, pl.ds(at, WIPE), :] = jnp.zeros((WIPE, LANES), jnp.float32)


    def spread(j, carry):
        def place(n, inner):
            wipe(inner)
            for k in range(PLACES):
                i = n * PLACES + k
                h = homes[j * blocks + i]
                n_h = filled[h]
                slots[h * cap + n_h] = j * each + i
                filled[h] = n_h + 1
            return inner + 1

        return lax.fori_loop(0, (counts[j] + PLACES - 1) // PLACES, place, carry)

    def wipe_rest(n, carry):
        wipe(n)
        return carry

    lax.fori_loop(lax.fori_loop(0, devices, spread, 0), wipes, wipe_rest, 0)

    def list_groups(h, found):
        count = filled[h]
        whole = (count + 1) // STACK

        def one(g, n):
            fours[3 * n] = h
            fours[3 * n + 1] = h * cap + STACK * g
            fours[3 * n + 2] = count - STACK * g
            return n + 1

        n, m = found
        n = lax.fori_loop(0, whole, one, n)
        rest = count - STACK * whole
        twos[3 * m] = h
        twos[3 * m + 1] = h * cap + STACK * whole
        twos[3 * m + 2] = rest
        return n, m + jnp.where(rest > 0, 1, 0)

    n_fours, n_twos = lax.fori_loop(0, half_tiles, list_groups, (0, 0))
    scale = 1.0 / math.sqrt(k_len)

    def prepare(batch, refs, stack, group, total):
        fine, coarse, signal, phase = refs
        for p in range(BATCH // stack):
            n = batch * (BATCH // stack) + p
            real = n < total
            n = jnp.where(real, n, 0)
            first = group[3 * n + 1]
            left_over = jnp.where(real, group[3 * n + 2], 0)
            for q in range(stack):
                live = q < left_over
                row = jnp.where(live, slots[first + q], 0)
                centre = (2 * cols[row] - (G - SUB + 1)).astype(jnp.float32)
                keep = jnp.where(live, scale, 0.0)
                k = p * stack + q
                signals = data_ref[row].astype(jnp.float32) * keep
                places = data_ref[row + blocks].astype(jnp.float32)
                for c in range(k_parts):
                    cut = slice(c * LANES, (c + 1) * LANES)
                    for r in range(2):
                        stage[r, c, k : k + 1, :] = signals[r : r + 1, cut]
                        stage[2 + r, c, k : k + 1, :] = places[r : r + 1, cut]
                stage[4, 0, k : k + 1, :] = jnp.full((1, LANES), centre, jnp.float32)
        for c in range(k_parts):
            halves = []
            for axis in range(2):
                turns = (stage[2 + axis, c] + 0.5) * (0.5 / SUB)
                half = cos_sin_part(turns, COS_S, SIN_S)
                halves.append(half)
                step = squared(half)
                power = half
                for b in range(8):
                    if b:
                        power = times(power, step)
                    for e in range(2):
                        fine[axis, e, c, b * 9 : b * 9 + 8, :] = power[e]
                power = squared(times(power, half))
                for e in range(2):
                    coarse[4 * axis + e, c] = power[e]
                power = squared(power)
                for e in range(2):
                    coarse[4 * axis + 2 + e, c] = power[e]
            hc, hs = times(*halves)
            vr, vi = stage[0, c], stage[1, c]
            signal[0, c] = vr * hc + vi * hs
            wi = vi * hc - vr * hs
            signal[1, c] = wi
            signal[2, c] = -wi
        for c in range(m_parts):
            pc, ps = cos_sin_turns(stage[4, 0] * m_ref[:, c * LANES : (c + 1) * LANES])
            phase[0, c] = pc
            phase[1, c] = ps
            phase[2, c] = -ps

    def expand(c, s, c1, s1, c2, s2):
        a, b, d, e = c1 * c, s1 * s, s1 * c, c1 * s
        return (
            jnp.concatenate([c, a + b, a - b, c2 * c + s2 * s], axis=0),
            jnp.concatenate([s, d - e, d + e, s2 * c - c2 * s], axis=0),
        )

    def piece_of(k, refs):
        fine, coarse, signal, _ = refs
        lefts, rights = [], []
        for c in range(k_parts):
            tables = []
            for axis in range(2):
                start = [fine[axis, e, c, pl.ds(k, 8, stride=9), :] for e in range(2)]
                rows = [coarse[4 * axis + n, c, k : k + 1, :] for n in range(4)]
                tables.append(expand(*start, *rows))
            (cu, su), (cv, sv) = tables
            wr, wi, nwi = (signal[n, c, k : k + 1, :] for n in range(3))
            lefts.append(
                jnp.concatenate([wr * cu, nwi * su, wi * cu, wr * su], axis=0).astype(jnp.bfloat16)
            )
            rights.append(jnp.concatenate([cv, sv], axis=0).astype(jnp.bfloat16))
        return lax.dot_general(
            jnp.concatenate(lefts, axis=1),
            jnp.concatenate(rights, axis=1),
            (((1,), (1,)), ((), ())),
            preferred_element_type=jnp.float32,
        ).astype(jnp.bfloat16)

    def gather_up(batch, refs, stack, group, total):
        phase = refs[3]
        pieces = [
            jnp.concatenate([piece_of(k, refs) for k in range(p * stack, (p + 1) * stack)], axis=1)
            for p in range(BATCH // stack)
        ]
        for p in range(BATCH // stack):
            n = batch * (BATCH // stack) + p
            h = group[3 * jnp.where(n < total, n, 0)]
            rows = pl.ds(h * PITCH, 2 * SUB)
            ks = range(p * stack, (p + 1) * stack)
            piece = pieces[p]
            wide = min(2, m_parts)
            for c0 in range(0, m_parts, wide):
                tops = [d_ref[:32, c * LANES : (c + 1) * LANES] for c in range(c0, c0 + wide)]
                lows = [d_ref[32:, c * LANES : (c + 1) * LANES] for c in range(c0, c0 + wide)]
                for turn in range(2):
                    weight = []
                    for k in ks:
                        top, low = [], []
                        for c in range(c0, c0 + wide):
                            pr, pi, npi = (phase[e, c, k : k + 1, :] for e in range(3))
                            top.append(tops[c - c0] * (pi if turn else pr))
                            low.append(lows[c - c0] * (pr if turn else npi))
                        weight += [jnp.concatenate(top, axis=1), jnp.concatenate(low, axis=1)]
                    got = jnp.dot(
                        piece,
                        jnp.concatenate(weight, axis=0).astype(jnp.bfloat16),
                        preferred_element_type=jnp.float32,
                    )
                    for c in range(wide):
                        at = turn * m_parts + c0 + c
                        acc[at, rows, :] += got[:, c * LANES : (c + 1) * LANES]

    for stack, group, total in ((STACK, fours, n_fours), (2, twos, n_twos)):
        batches = (total + BATCH // stack - 1) // (BATCH // stack)
        rest = (stack, group, total)
        prepare(0, sets[0], *rest)

        def step(it, carry, rest=rest):
            for n in range(2):
                gather_up(2 * it + n, sets[n], *rest)
                prepare(2 * it + n + 1, sets[1 - n], *rest)
            return carry

        lax.fori_loop(0, batches // 2, step, 0)

        def last(it, carry, rest=rest, batches=batches):
            gather_up(batches - 1, sets[0], *rest)
            return carry

        lax.fori_loop(0, lax.rem(batches, 2), last, 0)

    def turned(lam, carry):
        top = [acc[c, pl.ds(lam, half_tiles, stride=PITCH), :] for c in range(2 * m_parts)]
        low = [acc[c, pl.ds(SUB + lam, half_tiles, stride=PITCH), :] for c in range(2 * m_parts)]
        re = [top[c] - low[m_parts + c] for c in range(m_parts)]
        im = [top[m_parts + c] + low[c] for c in range(m_parts)]
        if width < LANES:
            re = [re[0][:, :width], re[0][:, width:]]
            im = [im[0][:, :width], im[0][:, width:]]
        whole = [jnp.concatenate(x, axis=0).astype(jnp.bfloat16) for x in zip(re, im)]
        parts = len(whole) // 2
        for c in range(parts):
            keep_ref[c, lam] = whole[c]
            give_ref[c, lam] = whole[parts + c]
        return carry

    lax.fori_loop(0, SUB, turned, 0, unroll=4)


def in_lanes(rows):
    width = rows.shape[1]
    if width < LANES:
        return [jnp.concatenate([rows] * (LANES // width), axis=1)]
    return [rows[:, c : c + LANES] for c in range(0, width, LANES)]


def lane_chunks(width):
    return max(1, width // LANES)


def tail_rows(width, share, place, y_of, table, out_t):
    part, depth, m_first = place

    def step(l0, carry):
        z = jnp.dot(table[l0], y_of(l0), preferred_element_type=jnp.float32)
        l1 = part * share + lax.broadcasted_iota(jnp.int32, (share, width), 0)
        l = l0 + 64 * l1 - G // 2
        m = m_first + lax.broadcasted_iota(jnp.int32, (share, width), 1)
        x = l.astype(jnp.float32) * (1.0 / G)
        y = m.astype(jnp.float32) * (1.0 / G)
        ramp = jnp.bitwise_and(-(G - SUB + 1) * l, 2 * G - 1).astype(jnp.float32) * (0.5 / G)
        sc, ss = cos_sin_turns(depth * (jnp.sqrt(1.0 - y * y - x * x) - 1.0) + ramp)
        for c, rows in enumerate(in_lanes(z[:, :width] * sc - z[:, width:] * ss)):
            out_t[c, pl.ds(l0, share, stride=64), :] = rows
        return carry

    lax.fori_loop(0, 64, step, 0, unroll=4)


def turn_out(out_t, out_ref):
    chunk = 128

    def step(n, carry):
        at = pl.multiple_of(n * chunk, chunk)
        for c in range(out_t.shape[0]):
            turned = out_t[c, pl.ds(at, chunk), :].T.astype(out_ref.dtype)
            width = min(LANES, out_ref.shape[0])
            out_ref[c * width : (c + 1) * width, pl.ds(at, chunk)] = turned[:width]
        return carry

    lax.fori_loop(0, out_t.shape[1] // chunk, step, 0, unroll=4)


def head_kernel(
    width, share, places, depths, own_ref, came_ref, head_ref, table, y_ref, out_ref, mid, out_t
):
    def head(lam, carry):
        rhs = jnp.concatenate([own_ref[0, lam], came_ref[0, lam]], axis=0)
        got = jnp.dot(head_ref[...], rhs, preferred_element_type=jnp.float32)
        for c, rows in enumerate(in_lanes(got)):
            mid[c, pl.ds(lam * PITCH, 128), :] = rows
        return carry

    lax.fori_loop(0, SUB, head, 0, unroll=4)

    def y_of(l0):
        halves = []
        for first in (0, 64):
            rows = [mid[c, pl.ds(first + l0, SUB, stride=PITCH), :] for c in range(mid.shape[0])]
            halves += [r[:, : min(width, LANES)] for r in rows]
        y = jnp.concatenate(halves, axis=1).astype(jnp.bfloat16)
        y_ref[l0] = y
        return y

    tail_rows(width, share, (places[0], depths[0], places[1]), y_of, table, out_t)
    turn_out(out_t, out_ref)


def tail_kernel(width, share, places, depths, y_ref, table, out_ref, out_t):
    tail_rows(
        width, share, (places[0], depths[0], places[1]), lambda l0: y_ref[l0], table, out_t
    )
    turn_out(out_t, out_ref)


def finish_kernel(
    width, places, depths, keep_ref, give_ref, head_all, table,
    out_ref, came, mid, y_buf, away, other, out_t, core_send, core_recv, far_send, far_recv,
):
    uv = lax.axis_index("uv")
    wa = lax.axis_index("wa")
    near = {"uv": uv + 1 - 2 * lax.rem(uv, 2)}
    far = {"wa": 1 - wa}
    mesh_type = pl.DeviceIdType.MESH
    barrier = pltpu.get_barrier_semaphore()
    pl.semaphore_signal(barrier, inc=1, device_id=near, device_id_type=mesh_type)
    pl.semaphore_signal(barrier, inc=1, device_id=far, device_id_type=mesh_type)
    pl.semaphore_wait(barrier, 2)

    parts = width // LANES
    lam_step = SUB // SWAPS
    swaps = []
    for c in range(parts):
        for k in range(SWAPS):
            at = pl.ds(k * lam_step, lam_step)
            n = c * SWAPS + k
            swaps.append(
                pltpu.make_async_remote_copy(
                    src_ref=give_ref.at[c, at],
                    dst_ref=came.at[c, at],
                    send_sem=core_send.at[n],
                    recv_sem=core_recv.at[n],
                    device_id=near,
                    device_id_type=mesh_type,
                )
            )
            swaps[-1].start()
    core = lax.rem(uv, 2)

    share = SUB // 2
    step = 64 // SENDS

    def screened(c, l0, part, z):
        l1 = part * share + lax.broadcasted_iota(jnp.int32, (share, LANES), 0)
        l = l0 + 64 * l1 - G // 2
        m = places[1] + c * LANES + lax.broadcasted_iota(jnp.int32, (share, LANES), 1)
        x = l.astype(jnp.float32) * (1.0 / G)
        y = m.astype(jnp.float32) * (1.0 / G)
        ramp = jnp.bitwise_and(-(G - SUB + 1) * l, 2 * G - 1).astype(jnp.float32) * (0.5 / G)
        sc, ss = cos_sin_turns(depths[0] * (jnp.sqrt(1.0 - y * y - x * x) - 1.0) + ramp)
        return z[:, :LANES] * sc - z[:, LANES:] * ss

    sends = []
    for c in range(parts):

        def head(lam, carry, c=c):
            rhs = jnp.concatenate([keep_ref[c, lam], came[c, lam]], axis=0)
            mid[c, pl.ds(lam * PITCH, 128), :] = jnp.dot(
                head_all[core], rhs, preferred_element_type=jnp.float32
            )
            return carry

        for k in range(SWAPS):
            swaps[c * SWAPS + k].wait_recv()
            lax.fori_loop(k * lam_step, (k + 1) * lam_step, head, 0, unroll=16)

        def away_rows(l0, carry, c=c):
            y = jnp.concatenate(
                [mid[c, pl.ds(first + l0, SUB, stride=PITCH), :] for first in (0, 64)], axis=1
            ).astype(jnp.bfloat16)
            y_buf[c, l0] = y
            z = jnp.dot(table[1 - wa, l0], y, preferred_element_type=jnp.float32)
            away[c, l0] = screened(c, l0, 1 - places[0], z).astype(jnp.bfloat16)
            return carry

        for k in range(SENDS):
            lax.fori_loop(k * step, (k + 1) * step, away_rows, 0, unroll=8)
            at = pl.ds(k * step, step)
            n = c * SENDS + k
            sends.append(
                pltpu.make_async_remote_copy(
                    src_ref=away.at[c, at],
                    dst_ref=other.at[c, at],
                    send_sem=far_send.at[n],
                    recv_sem=far_recv.at[n],
                    device_id=far,
                    device_id_type=mesh_type,
                )
            )
            sends[-1].start()

    for c in range(parts):

        def own_rows(l0, carry, c=c):
            z = jnp.dot(table[wa, l0], y_buf[c, l0], preferred_element_type=jnp.float32)
            out_t[c, pl.ds(l0, share, stride=OUT_PITCH), :] = screened(c, l0, places[0], z)
            return carry

        lax.fori_loop(0, 64, own_rows, 0, unroll=16)

    for c in range(parts):

        def add_rows(l0, carry, c=c):
            at = pl.ds(l0, share, stride=OUT_PITCH)
            out_t[c, at, :] += other[c, l0].astype(jnp.float32)
            return carry

        for k in range(SENDS):
            sends[c * SENDS + k].wait_recv()
            lax.fori_loop(k * step, (k + 1) * step, add_rows, 0, unroll=8)

        for n in range(share // 2):
            rows = [out_t[c, pl.ds((2 * n + h) * OUT_PITCH, 64), :] for h in range(2)]
            out_ref[c * LANES : (c + 1) * LANES, n * LANES : (n + 1) * LANES] = jnp.concatenate(
                rows, axis=0
            ).T
    for one in swaps + sends:
        one.wait_send()


def on_device(visibility, coords, tile_row, col_offset, live_count):
    uv_count = lax.axis_size("uv")
    wa_count = lax.axis_size("wa")
    uv_index = lax.axis_index("uv")
    wa_index = lax.axis_index("wa")
    blocks = visibility.shape[0]
    k_len = visibility.shape[2]
    width = G // uv_count
    core = jnp.mod(uv_index, 2)
    partner = uv_index + 1 - 2 * core
    m_first = uv_index * width - G // 2
    m_both = jnp.concatenate(
        [m_first + jnp.arange(width), partner * width + jnp.arange(width) - G // 2]
    )[None, :].astype(jnp.float32) * (0.5 / G)
    given = lax.optimization_barrier(
        jnp.concatenate([tile_row.reshape(1, blocks), col_offset.reshape(1, blocks)], axis=0)
    )
    numbers = jnp.stack(
        [
            given[0],
            given[1] // SUB,
            jnp.bitwise_and(given[1], SUB - 1),
            jnp.broadcast_to(live_count[0], (blocks,)),
        ]
    )
    numbers = jnp.pad(numbers, ((0, 0), (0, k_len - blocks))).astype(jnp.bfloat16)
    packed = jnp.concatenate([visibility, coords, numbers.reshape(2, 2, k_len)], axis=0)
    all_data = gather_all(packed, uv_count)
    numbers = all_data[:, 2 * blocks :, :, :blocks].reshape(uv_count, 4, blocks)
    numbers = numbers.astype(jnp.int32)
    tiles = numbers[:, 0]
    cols = numbers[:, 1] * SUB + numbers[:, 2]
    cols = jnp.pad(cols, ((0, 0), (0, blocks + 2))).reshape(-1)
    live = jnp.arange(blocks)[None, :] < numbers[:, 3]
    mine = live & (jnp.mod(tiles, 2) == core)
    homes = jnp.where(mine, tiles // 2, G // SUB // 2).reshape(-1)
    half_tiles = G // SUB // 2
    cap = 2 * uv_count
    shape = (lane_chunks(width), SUB, SUB, min(width, LANES))
    vmem = pl.BlockSpec(memory_space=pltpu.VMEM)
    smem = pl.BlockSpec(memory_space=pltpu.SMEM)
    m_parts = 2 * width // LANES
    k_parts = k_len // LANES
    buffers = [
        pltpu.VMEM((2, 2, k_parts, 72, LANES), jnp.float32),
        pltpu.VMEM((8, k_parts, BATCH, LANES), jnp.float32),
        pltpu.VMEM((3, k_parts, BATCH, LANES), jnp.float32),
        pltpu.VMEM((3, m_parts, BATCH, LANES), jnp.float32),
    ]
    own, give = pl.pallas_call(
        functools.partial(grid_kernel, width, blocks),
        out_shape=[jax.ShapeDtypeStruct(shape, jnp.bfloat16)] * 2,
        in_specs=[smem, smem, smem, vmem, vmem, vmem],
        out_specs=[vmem, vmem],
        scratch_shapes=[
            pltpu.VMEM((2 * m_parts, -(-half_tiles * PITCH // WIPE) * WIPE, LANES), jnp.float32),
            pltpu.SMEM((half_tiles * cap + uv_count * blocks,), jnp.int32),
            pltpu.SMEM((half_tiles + 1,), jnp.int32),
            pltpu.SMEM((3 * (uv_count * blocks // STACK + half_tiles),), jnp.int32),
            pltpu.SMEM((3 * (half_tiles + 1),), jnp.int32),
            pltpu.VMEM((SUB, 2 * width), jnp.float32),
            pltpu.VMEM((5, k_parts, BATCH, LANES), jnp.float32),
        ]
        + buffers
        + buffers,
        compiler_params=pltpu.CompilerParams(vmem_limit_bytes=32 * 1024 * 1024),
    )(
        homes,
        cols,
        numbers[:, 3, 0],
        all_data.reshape((-1,) + all_data.shape[2:]),
        m_both,
        jnp.asarray(column_table(uv_count)),
    )
    share = 64 // wa_count
    depth = ((wa_index.astype(jnp.float32) - (wa_count - 1) / 2.0) * plane_step)[None]
    tables = jnp.asarray(row_table(wa_count))
    span = G // wa_count

    def places_of(part):
        return jnp.stack([part, m_first]).astype(jnp.int32)

    def head_of(part, dtype):
        return pl.pallas_call(
            functools.partial(head_kernel, width, share),
            out_shape=[
                jax.ShapeDtypeStruct((64, SUB, 2 * width), jnp.bfloat16),
                jax.ShapeDtypeStruct((width, span), dtype),
            ],
            in_specs=[smem, smem, vmem, vmem, vmem, vmem],
            out_specs=[vmem, vmem],
            scratch_shapes=[
                pltpu.VMEM((lane_chunks(width), SUB * PITCH, LANES), jnp.float32),
                pltpu.VMEM((lane_chunks(width), span, LANES), jnp.float32),
            ],
            compiler_params=pltpu.CompilerParams(vmem_limit_bytes=40 * 1024 * 1024),
        )(
            places_of(part), depth, own, came_half, jnp.asarray(head_matrices())[core], tables[part]
        )

    def tail_of(part, first, dtype):
        return pl.pallas_call(
            functools.partial(tail_kernel, width, share),
            out_shape=jax.ShapeDtypeStruct((width, span), dtype),
            in_specs=[smem, smem, vmem, vmem],
            out_specs=vmem,
            scratch_shapes=[pltpu.VMEM((lane_chunks(width), span, LANES), jnp.float32)],
            compiler_params=pltpu.CompilerParams(vmem_limit_bytes=40 * 1024 * 1024),
        )(places_of(part), depth, first, tables[part])

    if wa_count == 2 and width % LANES == 0:
        parts = width // LANES
        scratch = [
            pltpu.VMEM(shape, jnp.bfloat16),
            pltpu.VMEM((parts, SUB * PITCH, LANES), jnp.float32),
            pltpu.VMEM((parts, 64, SUB, 2 * LANES), jnp.bfloat16),
            pltpu.VMEM((parts, 64, share, LANES), jnp.bfloat16),
            pltpu.VMEM((parts, 64, share, LANES), jnp.bfloat16),
            pltpu.VMEM((parts, share * OUT_PITCH, LANES), jnp.float32),
        ]
        scratch += [pltpu.SemaphoreType.DMA((parts * SWAPS,))] * 2
        scratch += [pltpu.SemaphoreType.DMA((parts * SENDS,))] * 2
        return pl.pallas_call(
            functools.partial(finish_kernel, width),
            out_shape=jax.ShapeDtypeStruct((width, span), jnp.float32),
            in_specs=[smem, smem] + [vmem] * 4,
            out_specs=vmem,
            scratch_shapes=scratch,
            compiler_params=pltpu.CompilerParams(
                collective_id=1, has_side_effects=True, vmem_limit_bytes=24 * 1024 * 1024
            ),
        )(
            places_of(wa_index),
            depth,
            own,
            give,
            jnp.asarray(head_matrices()),
            tables,
        )
    came_half = lax.ppermute(give, "uv", [(n, n ^ 1) for n in range(uv_count)])

    first, part = head_of(jnp.int32(0), jnp.bfloat16)
    images = [part] + [tail_of(jnp.int32(n), first, jnp.bfloat16) for n in range(1, wa_count)]
    parts = jnp.stack(images, axis=1)
    came = lax.all_to_all(parts, "wa", split_axis=1, concat_axis=1)
    return jnp.sum(came.astype(jnp.float32), axis=1)


def solution(mesh):
    in_specs = (
        P(("wa", "uv"), None, None),
        P(("wa", "uv"), None, None),
        P(("wa", "uv"), None),
        P(("wa", "uv")),
        P("wa", "uv"),
    )
    return jax.shard_map(
        on_device, mesh=mesh, in_specs=in_specs, out_specs=P("uv", "wa"), check_vma=False
    )
```
